32 devices in a mesh: cluster: 8 (over z, x), narrow: 4 (over y, core).
Axes of the slice: x: 2, y: 2, z: 4, core: 2. Of those that a mesh axis runs over, the one named last changes fastest.
Arguments:
- edge_feats: bfloat16 [65536, 512], P(('cluster', 'narrow')), may hold values from -6 to 6
- cotangent: bfloat16 [65536, 512], P(('cluster', 'narrow')), may hold values from -6 to 6
- down_weight: bfloat16 [512, 64], replicated, may hold values from -0.25 to 0.25
- up_weight: bfloat16 [64, 512], replicated, may hold values from -0.75 to 0.75
- inner_weight: bfloat16 [1, 512, 512], replicated, may hold values from -0.25 to 0.25
- outer_weight: bfloat16 [1, 512, 512], replicated, may hold values from -0.25 to 0.25
- angular: bfloat16 [1024, 8, 4096], P(('cluster', 'narrow')), may hold values from -0.375 to 0.375
- reverse: int32 [65536], P(('cluster', 'narrow')), may hold values from 0 to 65535, as said below
- sources: int32 [1024, 8], P(('cluster', 'narrow')), may hold values from 0 to 1023, as said below
- counts: int32 [1024], P(('cluster', 'narrow')), may hold values from 1 to 8
Outputs:
- output: bfloat16 [65536, 512], P(('cluster', 'narrow'))
- grad_x: bfloat16 [65536, 512], P(('cluster', 'narrow'))
The draws below stay inside these ranges and needn't reach their ends.
Inputs may be any that keep to these rules, and one draw needn't show every extreme that they name: reverse is an involution without fixed points, and reverse[e] // 2048 == ((e + 32768) % 65536) // 2048. sources[k, s] // 128 == k // 128; among the slots of the blocks of one device (blocks m * 32 to (m + 1) * 32 - 1), exactly 64 name a block j with (j % 128) // 32 == i, for every i below 4; slots s >= counts[k] hold valid block numbers that are not used.
All inputs are finite; a program needn't handle non-finite values.
Results may differ from the reference program's by a relative error of at most 0.0075.
Values may be sent and summed in bfloat16 or wider, within the bound.
No kernel may reach another device: no remote copies, remote signals or barrier semaphores. Data moves between devices by JAX's collectives and lax.ppermute only.
A program may use at most 128 MiB of HBM per device.

```python
import jax
import jax.numpy as jnp
from jax import lax

D = 512
TRIP = 64
BLK = 64
SEL = 8
RES = 1
E_DEV = 2048
EDGES = 65536
BLOCKS = 1024
CL_BLOCKS = 128
HALF = 32768
PAIRS = 16


def draw_reverse(key, part):
    pair_keys = jax.random.split(key, PAIRS)
    shuffles = jax.vmap(lambda subkey: jax.random.permutation(subkey, E_DEV))(pair_keys).astype(jnp.int32)
    inverse = jnp.argsort(shuffles, axis=1).astype(jnp.int32)
    pair_base = jnp.arange(PAIRS, dtype=jnp.int32)[:, None] * E_DEV
    lower_half = pair_base + shuffles + HALF
    upper_half = pair_base + inverse
    return jnp.concatenate([lower_half.reshape(-1), upper_half.reshape(-1)]).astype(jnp.int32)


def draw_sources(key, part):
    per_device = E_DEV // BLK
    device_count = BLOCKS // per_device
    slot_total = per_device * SEL
    lane_total = CL_BLOCKS // per_device
    perm_keys = jax.random.split(jax.random.fold_in(key, 3), device_count)
    shuffles = jax.vmap(lambda subkey: jax.random.permutation(subkey, slot_total))(perm_keys).astype(jnp.int32)
    lanes = shuffles % lane_total
    within = jax.random.randint(jax.random.fold_in(key, 5), (device_count, slot_total), 0, per_device).astype(jnp.int32)
    device_ids = jnp.arange(device_count, dtype=jnp.int32)[:, None]
    base_block = device_ids * per_device // CL_BLOCKS * CL_BLOCKS
    chosen = base_block + lanes * per_device + within
    return chosen.reshape(BLOCKS, SEL).astype(jnp.int32)


def draw_counts(key, part):
    per_device = E_DEV // BLK
    level_key = jax.random.fold_in(key, 7)
    count_key = jax.random.fold_in(key, 11)
    levels = jax.random.randint(level_key, (BLOCKS // per_device, 1), 1, SEL + 1).astype(jnp.int32)
    levels = jnp.broadcast_to(levels, (BLOCKS // per_device, per_device)).reshape(BLOCKS)
    drawn = jax.random.randint(count_key, (BLOCKS,), 1, levels + 1).astype(jnp.int32)
    drawn = drawn.at[0].set(SEL)
    drawn = drawn.at[1].set(1)
    return drawn.astype(jnp.int32)


def block_scale(stream_key, shape, cuts, smallest, largest):
    def one(axis_at, parts):
        draws = jax.random.uniform(jax.random.fold_in(jax.random.fold_in(stream_key, 6), axis_at), (parts,), jnp.float32, smallest / len(cuts), largest / len(cuts))
        return jnp.repeat(jnp.exp(draws), shape[axis_at] // parts).reshape((-1,) + (1,) * (len(shape) - axis_at - 1))

    gain = one(*cuts[0])
    for cut in cuts[1:]:
        gain = gain * one(*cut)
    return gain


def normal_values(rng, extent, width, limit, shards=(), kind=jnp.bfloat16):
    array = jax.random.normal(rng, extent, jnp.float32) * width
    if len(shards) > 0:
        array = block_scale(rng, extent, shards, -0.22, 0.18) * array
    return jnp.clip(array, min=-limit, max=limit).astype(kind)


def setup_inputs(seed: int = 0) -> dict:
    arg_keys = jax.random.split(jax.random.key(seed), 11)
    return {
        "edge_feats": normal_values(arg_keys[0], (EDGES, D), 1.0, 6.0, ((0, 32),)),
        "cotangent": normal_values(arg_keys[1], (EDGES, D), 1.0, 6.0, ((0, 32),)),
        "down_weight": normal_values(arg_keys[2], (D, TRIP), D ** -0.5, 0.25),
        "up_weight": normal_values(arg_keys[3], (TRIP, D), TRIP ** -0.5, 0.75),
        "inner_weight": normal_values(arg_keys[4], (RES, D, D), D ** -0.5, 0.25),
        "outer_weight": normal_values(arg_keys[5], (RES, D, D), D ** -0.5, 0.25),
        "angular": normal_values(arg_keys[6], (BLOCKS, SEL, BLK * BLK), (BLK * 4) ** -0.5, 0.375, ((0, 32),)),
        "reverse": draw_reverse(jax.random.fold_in(arg_keys[10], 71), 0),
        "sources": draw_sources(jax.random.fold_in(arg_keys[10], 71), 0),
        "counts": draw_counts(jax.random.fold_in(arg_keys[10], 71), 0),
    }


ROOT_HALF = 0.7071067811865476

def silu_grad(pre_act):
    squash = jax.nn.sigmoid(pre_act)
    return squash * (1.0 + pre_act * (1.0 - squash))

def reference(edge_feats, cotangent, down_weight, up_weight, inner_weight, outer_weight, angular, reverse, sources, counts):
    per_group = E_DEV // BLK
    group_count = BLOCKS // per_group
    pre_down = jnp.dot(edge_feats, down_weight, preferred_element_type=jnp.float32)
    trip_feat = jax.nn.silu(pre_down).astype(jnp.bfloat16)
    trip_blocks = trip_feat.reshape(BLOCKS, BLK * TRIP)
    live_mask = (lax.broadcasted_iota(jnp.int32, (BLOCKS, SEL), 1) < counts[:, None]).astype(jnp.float32)
    angle_groups = angular.reshape(group_count, per_group, SEL, BLK, BLK)
    source_groups = sources.reshape(group_count, per_group, SEL)
    mask_groups = live_mask.reshape(group_count, per_group, SEL)

    def forward_group(inputs):
        angle_mats, source_ids, mask_part = inputs
        picked = trip_blocks[source_ids].astype(jnp.float32) * mask_part[:, :, None]
        picked = picked.reshape(per_group, SEL, BLK, TRIP)
        return jnp.einsum('ksij,ksjf->kif', angle_mats.astype(jnp.float32), picked)
    trip_sum = lax.map(forward_group, (angle_groups, source_groups, mask_groups)).reshape(EDGES, TRIP)
    trip_round = trip_sum.astype(jnp.bfloat16)
    pre_up = jnp.dot(trip_round, up_weight, preferred_element_type=jnp.float32)
    up_feat = jax.nn.silu(pre_up).astype(jnp.bfloat16)
    message = (up_feat.astype(jnp.float32) + up_feat[reverse].astype(jnp.float32)) * ROOT_HALF
    hidden_state = (edge_feats.astype(jnp.float32) + message) * ROOT_HALF
    saved_acts = []
    for layer_index in range(RES):
        state_round = hidden_state.astype(jnp.bfloat16)
        pre_in = jnp.dot(state_round, inner_weight[layer_index], preferred_element_type=jnp.float32)
        act_feat = jax.nn.silu(pre_in).astype(jnp.bfloat16)
        pre_out = jnp.dot(act_feat, outer_weight[layer_index], preferred_element_type=jnp.float32)
        saved_acts.append((pre_in, pre_out))
        hidden_state = (hidden_state + jax.nn.silu(pre_out)) * ROOT_HALF
    output = hidden_state.astype(jnp.bfloat16)
    grad_state = cotangent.astype(jnp.float32)
    for layer_index in reversed(range(RES)):
        pre_in, pre_out = saved_acts[layer_index]
        grad_state = grad_state * ROOT_HALF
        grad_out = (grad_state * silu_grad(pre_out)).astype(jnp.bfloat16)
        grad_act = jnp.dot(grad_out, outer_weight[layer_index].T, preferred_element_type=jnp.float32)
        grad_in = (grad_act * silu_grad(pre_in)).astype(jnp.bfloat16)
        grad_state = grad_state + jnp.dot(grad_in, inner_weight[layer_index].T, preferred_element_type=jnp.float32)
    grad_msg = grad_state * ROOT_HALF
    grad_msg_round = grad_msg.astype(jnp.bfloat16)
    grad_up = (grad_msg + grad_msg_round[reverse].astype(jnp.float32)) * ROOT_HALF
    grad_pre_up = (grad_up * silu_grad(pre_up)).astype(jnp.bfloat16)
    grad_trip = jnp.dot(grad_pre_up, up_weight.T, preferred_element_type=jnp.float32).astype(jnp.bfloat16)
    grad_groups = grad_trip.reshape(group_count, per_group, BLK, TRIP)

    def backward_group(accumulated, inputs):
        angle_mats, source_ids, mask_part, grad_part = inputs
        pair_terms = jnp.einsum('ksij,kif->ksjf', angle_mats.astype(jnp.float32), grad_part.astype(jnp.float32))
        pair_terms = pair_terms * mask_part[:, :, None, None]
        accumulated = accumulated.at[source_ids.reshape(-1)].add(pair_terms.reshape(per_group * SEL, BLK * TRIP))
        return (accumulated, None)
    source_grad, ignored = lax.scan(backward_group, jnp.zeros((BLOCKS, BLK * TRIP), jnp.float32), (angle_groups, source_groups, mask_groups, grad_groups))
    source_grad = source_grad.reshape(EDGES, TRIP)
    grad_pre_down = (source_grad * silu_grad(pre_down)).astype(jnp.bfloat16)
    grad_x = grad_msg + jnp.dot(grad_pre_down, down_weight.T, preferred_element_type=jnp.float32)
    return (output, grad_x.astype(jnp.bfloat16))
```

```python
import functools

import jax
import jax.numpy as jnp
from jax import lax
from jax.experimental import pallas as pl
from jax.experimental.pallas import tpu as pltpu
from jax.sharding import PartitionSpec as P

ROOT_HALF = 0.7071067811865476
MIB = 1 << 20
F32 = jnp.float32
BF16 = jnp.bfloat16


def dot(left, right):
    return jnp.dot(left, right, preferred_element_type=F32)


def dot_trans(left, right):
    return lax.dot_general(left, right, (((1,), (1,)), ((), ())), preferred_element_type=F32)


def sigmoid(value):
    return 0.5 * jnp.tanh(0.5 * value) + 0.5


def swapped(array, axis, bit):
    return lax.ppermute(array, axis, [(i, i ^ bit) for i in range(lax.axis_size(axis))])


def half_mask(shape, width):
    return lax.broadcasted_iota(jnp.int32, shape, 1) < width


def split_pairs(rows, block):
    parts = rows.reshape(-1, 2, block, rows.shape[-1])
    return parts[:, 0].reshape(-1, rows.shape[-1]), parts[:, 1].reshape(-1, rows.shape[-1])


def join_pairs(even, odd, block):
    width = even.shape[-1]
    both = jnp.concatenate([even.reshape(-1, 1, block, width), odd.reshape(-1, 1, block, width)], axis=1)
    return both.reshape(-1, width)


def params(limit, **more):
    return pltpu.CompilerParams(vmem_limit_bytes=limit, **more)


def down_kernel(block, x_ref, wl_ref, wr_ref, pre_ref, trip_ref):
    even, odd = split_pairs(x_ref[...], block)
    pre = dot(even, wl_ref[...]) + dot(odd, wr_ref[...])
    pre_ref[...] = pre
    trip_ref[...] = (pre * sigmoid(pre)).astype(BF16)


def down(x, wl, wr, block, steps):
    rows, width = x.shape
    lanes = wl.shape[1]
    return pl.pallas_call(
        functools.partial(down_kernel, block),
        grid=(steps,),
        in_specs=[
            pl.BlockSpec((rows // steps, width), lambda i: (i, 0)),
            pl.BlockSpec((width, lanes), lambda i: (0, 0)),
            pl.BlockSpec((width, lanes), lambda i: (0, 0)),
        ],
        out_specs=[pl.BlockSpec((rows // 2 // steps, lanes), lambda i: (i, 0))] * 2,
        out_shape=[
            jax.ShapeDtypeStruct((rows // 2, lanes), F32),
            jax.ShapeDtypeStruct((rows // 2, lanes), BF16),
        ],
        compiler_params=params(32 * MIB),
        name="down",
    )(x, wl, wr)


def triplet_kernel(block, slots, pieces, *refs):
    index_ref, code_ref, angle_ref = refs[:3]
    piece_refs = refs[3 : 3 + pieces]
    trip_ref, sent_ref, left_ref, right_ref, dup_ref = refs[3 + pieces :]
    packed_rows, lanes = trip_ref.shape
    half = lanes // 2
    groups = packed_rows // block
    zero = jnp.zeros((block, lanes), BF16)
    left_ref[pieces * groups * 2] = zero
    right_ref[pieces * groups * 2] = zero
    mask = half_mask((block, lanes), half)

    for piece in range(pieces):

        def spread(m, carry, piece=piece):
            rows = piece_refs[piece][pl.ds(pl.multiple_of(m * block, block), block), :].astype(F32)
            other = pltpu.roll(rows, half, 1)
            at = (piece * groups + m) * 2
            left_ref[at] = jnp.where(mask, rows, 0.0).astype(BF16)
            left_ref[at + 1] = jnp.where(mask, other, 0.0).astype(BF16)
            right_ref[at] = jnp.where(mask, 0.0, other).astype(BF16)
            right_ref[at + 1] = jnp.where(mask, 0.0, rows).astype(BF16)
            return carry

        lax.fori_loop(0, groups, spread, 0, unroll=4)

    def target(m, carry):
        base = m * (2 * slots)
        picked = [left_ref[index_ref[base + s]] for s in range(slots)]
        picked += [right_ref[index_ref[base + slots + s]] for s in range(slots)]
        total = dot(angle_ref[m], jnp.concatenate(picked, axis=0))
        at = pl.ds(pl.multiple_of(m * block, block), block)
        trip_ref[at, :] = total.astype(BF16)
        rounded = total.astype(BF16).astype(F32)
        other = pltpu.roll(rounded, half, 1)
        dup_ref[0, at, :] = jnp.where(mask, rounded, other).astype(BF16)
        dup_ref[1, at, :] = jnp.where(mask, other, rounded).astype(BF16)
        return carry

    lax.fori_loop(0, groups, target, 0, unroll=2)

    every = dup_ref[...].reshape(2 * packed_rows, lanes)
    code = code_ref[...]
    tile = 2 * block
    tile_mask = half_mask((tile, lanes), half)

    def send(t, carry):
        def part(base):
            spot = lax.broadcasted_iota(jnp.int32, (tile, 2 * packed_rows), 0) + (base + t * tile)
            return dot((spot == code).astype(F32).astype(BF16), every)

        both = jnp.where(tile_mask, part(0), part(packed_rows))
        sent_ref[pl.ds(pl.multiple_of(t * tile, tile), tile), :] = both.astype(BF16)
        return carry

    lax.fori_loop(0, packed_rows // tile, send, 0, unroll=2)


def triplet(index, code, angles, pieces, block, slots):
    packed_rows, lanes = pieces[0].shape
    blocks = packed_rows // block * 2 * len(pieces)
    vmem = pl.BlockSpec(memory_space=pltpu.VMEM)
    return pl.pallas_call(
        functools.partial(triplet_kernel, block, slots, len(pieces)),
        in_specs=[pl.BlockSpec(memory_space=pltpu.SMEM)] + [vmem] * (2 + len(pieces)),
        out_specs=[vmem] * 2,
        out_shape=[jax.ShapeDtypeStruct((packed_rows, lanes), BF16)] * 2,
        scratch_shapes=[
            pltpu.VMEM((blocks + 1, block, lanes), BF16),
            pltpu.VMEM((blocks + 1, block, lanes), BF16),
            pltpu.VMEM((2, packed_rows, lanes), BF16),
        ],
        compiler_params=params(48 * MIB),
        name="triplet",
    )(index, code, angles, *pieces)


def layer_kernel(
    block, x_ref, ct_ref, own_ref, far_ref, up2_ref, upl_ref, upr_ref, wi_ref, wo_ref, *refs
):
    out_ref, grad_ref, near_ref, send_ref = refs[-4:]
    lanes = own_ref.shape[1]
    up2 = up2_ref[...]
    mask = half_mask(own_ref.shape, lanes // 2)
    none = jnp.zeros(own_ref.shape, BF16)

    def pre_up(ref):
        rows = ref[...]
        return dot(join_pairs(jnp.where(mask, rows, none), jnp.where(mask, none, rows), block), up2)

    def gated(pre):
        squash = sigmoid(pre)
        value = pre * squash
        return value, squash + value * (1.0 - squash)

    own_value, own_slope = gated(pre_up(own_ref))
    far_value, far_slope = gated(pre_up(far_ref))
    message = (own_value.astype(BF16).astype(F32) + far_value.astype(BF16).astype(F32)) * ROOT_HALF
    hidden = (x_ref[...].astype(F32) + message) * ROOT_HALF
    wi, wo = wi_ref[...], wo_ref[...]
    in_value, in_slope = gated(dot(hidden.astype(BF16), wi))
    out_value, out_slope = gated(dot(in_value.astype(BF16), wo))
    out_ref[...] = ((hidden + out_value) * ROOT_HALF).astype(BF16)
    scaled = ct_ref[...].astype(F32) * ROOT_HALF
    grad_out = (scaled * out_slope).astype(BF16)
    grad_in = (dot_trans(grad_out, wo) * in_slope).astype(BF16)
    grad_msg = (scaled + dot_trans(grad_in, wi)) * ROOT_HALF
    grad_round = grad_msg.astype(BF16)
    grad_ref[...] = grad_round

    def project(rows):
        even, odd = split_pairs(rows.astype(BF16), block)
        return (dot_trans(even, upl_ref[...]) + dot_trans(odd, upr_ref[...])) * ROOT_HALF

    near_ref[...] = project(grad_msg * own_slope)
    send_ref[...] = project(grad_round.astype(F32) * far_slope).astype(BF16)


def layer(x, ct, own, far, up2, upl, upr, wi, wo, block, steps):
    rows, width = x.shape
    lanes = own.shape[1]
    whole = lambda array: pl.BlockSpec(array.shape, lambda i: (0, 0))
    wide = pl.BlockSpec((rows // steps, width), lambda i: (i, 0))
    thin = pl.BlockSpec((rows // 2 // steps, lanes), lambda i: (i, 0))
    return pl.pallas_call(
        functools.partial(layer_kernel, block),
        grid=(steps,),
        in_specs=[wide, wide, thin, thin] + [whole(w) for w in (up2, upl, upr, wi, wo)],
        out_specs=[wide, wide, thin, thin],
        out_shape=[
            jax.ShapeDtypeStruct((rows, width), BF16),
            jax.ShapeDtypeStruct((rows, width), BF16),
            jax.ShapeDtypeStruct((rows // 2, lanes), F32),
            jax.ShapeDtypeStruct((rows // 2, lanes), BF16),
        ],
        compiler_params=params(48 * MIB),
        name="layer",
    )(x, ct, own, far, up2, upl, upr, wi, wo)


def scatter_kernel(block, slots, pieces, index_ref, row_ref, angle_ref, near_ref, far_ref, *refs):
    out_refs = refs[:pieces]
    total_ref, grad_ref = refs[pieces:]
    packed_rows, lanes = near_ref.shape
    half = lanes // 2
    groups = packed_rows // block
    mask = half_mask((block, lanes), half)
    total_ref[...] = jnp.zeros(total_ref.shape, F32)
    far = far_ref[...]
    tile = 2 * block
    tile_mask = half_mask((tile, lanes), half)

    def collect(m, carry):
        rows = row_ref[pl.ds(pl.multiple_of(m * tile, tile), tile), :]
        spot = lax.broadcasted_iota(jnp.int32, (tile, packed_rows), 1)
        got = dot((spot == (rows & (packed_rows - 1))).astype(F32).astype(BF16), far)
        got = jnp.where(tile_mask == (rows < packed_rows), got, 0.0)
        got = got + pltpu.roll(got, half, 1)
        both = jnp.where(mask, got[:block], got[block:])
        at = pl.ds(pl.multiple_of(m * block, block), block)
        grad_ref[at, :] = (near_ref[at, :] + both).astype(BF16)
        return carry

    lax.fori_loop(0, groups, collect, 0, unroll=2)
    none = jnp.zeros((block, lanes), BF16)

    def target(m, carry):
        rows = grad_ref[pl.ds(pl.multiple_of(m * block, block), block), :]
        pair = jnp.concatenate([jnp.where(mask, rows, none), jnp.where(mask, none, rows)], axis=0)
        terms = dot(angle_ref[m], pair)
        base = m * (2 * slots)
        for s in range(slots):
            term = terms[s * block : (s + 1) * block]
            total_ref[index_ref[base + s]] += jnp.where(mask, term, 0.0)
            total_ref[index_ref[base + slots + s]] += jnp.where(mask, 0.0, term)
        return carry

    lax.fori_loop(0, groups, target, 0)

    for piece in range(pieces):

        def finish(m, carry, piece=piece):
            at = piece * groups + m
            total = total_ref[at] + pltpu.roll(total_ref[pieces * groups + at], half, 1)
            rows = pl.ds(pl.multiple_of(m * block, block), block)
            out_refs[piece][rows, :] = total.astype(out_refs[piece].dtype)
            return carry

        lax.fori_loop(0, groups, finish, 0, unroll=2)


def scatter(index, row, angles, near, far, types, block, slots):
    packed_rows, lanes = near.shape
    pieces = len(types)
    groups = packed_rows // block
    vmem = pl.BlockSpec(memory_space=pltpu.VMEM)
    return pl.pallas_call(
        functools.partial(scatter_kernel, block, slots, pieces),
        in_specs=[pl.BlockSpec(memory_space=pltpu.SMEM)] + [vmem] * 4,
        out_specs=[vmem] * pieces,
        out_shape=[jax.ShapeDtypeStruct((packed_rows, lanes), kind) for kind in types],
        scratch_shapes=[
            pltpu.VMEM((2 * pieces * groups + 1, block, lanes), F32),
            pltpu.VMEM((packed_rows, lanes), BF16),
        ],
        compiler_params=params(56 * MIB),
        name="scatter",
    )(index, row, angles, near, far)


def last_kernel(block, pre_ref, grad_ref, wl_ref, wr_ref, *refs):
    out_ref = refs[-1]
    total = refs[0][...].astype(F32)
    for ref in refs[1:-1]:
        total = total + ref[...].astype(F32)
    pre = pre_ref[...]
    squash = sigmoid(pre)
    grad = (total * (squash + pre * squash * (1.0 - squash))).astype(BF16)
    both = join_pairs(dot_trans(grad, wl_ref[...]), dot_trans(grad, wr_ref[...]), block)
    out_ref[...] = (grad_ref[...].astype(F32) + both).astype(BF16)


def last(pre, grad_msg, wl, wr, terms, block, steps):
    rows, width = grad_msg.shape
    lanes = wl.shape[1]
    wide = pl.BlockSpec((rows // steps, width), lambda i: (i, 0))
    thin = pl.BlockSpec((rows // 2 // steps, lanes), lambda i: (i, 0))
    weight = pl.BlockSpec((width, lanes), lambda i: (0, 0))
    return pl.pallas_call(
        functools.partial(last_kernel, block),
        grid=(steps,),
        in_specs=[thin, wide, weight, weight] + [thin] * len(terms),
        out_specs=wide,
        out_shape=jax.ShapeDtypeStruct((rows, width), BF16),
        compiler_params=params(32 * MIB),
        name="last",
    )(pre, grad_msg, wl, wr, *terms)


def on_device(
    edge_feats,
    cotangent,
    down_weight,
    up_weight,
    inner_weight,
    outer_weight,
    angular,
    reverse,
    sources,
    counts,
):
    lane_count = lax.axis_size("narrow")
    top_bit = lax.axis_size("cluster") // 2
    me = lax.axis_index("narrow")
    local_blocks, slots = sources.shape
    local_edges = edge_feats.shape[0]
    block = local_edges // local_blocks
    groups = local_blocks // 2
    packed_rows = local_edges // 2
    width = down_weight.shape[1]

    none = jnp.zeros_like(down_weight)
    wl = jnp.concatenate([down_weight, none], axis=1)
    wr = jnp.concatenate([none, down_weight], axis=1)
    up_none = jnp.zeros_like(up_weight)
    up2 = jnp.concatenate([up_weight, up_weight], axis=0)
    upl = jnp.concatenate([up_weight, up_none], axis=0).T
    upr = jnp.concatenate([up_none, up_weight], axis=0).T
    upl, upr = upl.T, upr.T

    live = lax.broadcasted_iota(jnp.int32, sources.shape, 1) < counts[:, None]
    local = sources % (local_blocks * lane_count)
    spot = (local // local_blocks ^ me) * local_blocks + local % local_blocks
    forward_index = jnp.where(live, spot, lane_count * local_blocks).reshape(-1)
    odd = lax.broadcasted_iota(jnp.int32, sources.shape, 0) % 2
    turned = jnp.where(spot % 2 == odd, 0, lane_count * groups)
    backward_index = jnp.where(live, turned + spot // 2, 2 * lane_count * groups).reshape(-1)

    slot = reverse % local_edges
    place = (slot // block % 2) * packed_rows + slot // (2 * block) * block + slot % block
    code = place.reshape(groups, 2, block).transpose(1, 0, 2).reshape(1, local_edges)

    angles = angular.reshape(groups, 2, slots, block, block)
    angle_in = angles.transpose(0, 3, 1, 2, 4).reshape(groups, block, 2 * slots * block)
    angle_out = angles.transpose(0, 2, 4, 1, 3).reshape(groups, slots * block, 2 * block)

    pre_down, trip = down(edge_feats, wl, wr, block, 4)
    pieces = {0: trip}
    bits = [1 << i for i in range(lane_count.bit_length() - 1)]
    for bit in reversed(bits):
        pieces.update({d ^ bit: swapped(piece, "narrow", bit) for d, piece in pieces.items()})
    trip_own, trip_sent = triplet(
        forward_index, code, angle_in, [pieces[d] for d in range(lane_count)], block, slots
    )
    trip_far = swapped(trip_sent, "cluster", top_bit)
    output, grad_msg, near, sent = layer(
        edge_feats,
        cotangent,
        trip_own,
        trip_far,
        up2,
        upl,
        upr,
        inner_weight[0],
        outer_weight[0],
        block,
        8,
    )
    far = swapped(sent, "cluster", top_bit)
    types = [BF16 if d % 2 else F32 for d in range(lane_count)]
    parts = scatter(backward_index, place.reshape(local_edges, 1), angle_out, near, far, types, block, slots)
    parts = dict(enumerate(parts))
    terms = [parts[0]]
    for bit in bits:
        for d in range(lane_count - bit, -1, -2 * bit):
            got = swapped(parts[d].astype(BF16), "narrow", bit)
            if d == bit:
                terms.append(got)
            else:
                parts[d ^ bit] = parts[d ^ bit] + got.astype(F32)
    grad_x = last(pre_down, grad_msg, wl, wr, terms, block, 4)
    return (output, grad_x)


def solution(mesh):
    in_specs = (
        P(("cluster", "narrow"), None),
        P(("cluster", "narrow"), None),
        P(),
        P(),
        P(),
        P(),
        P(("cluster", "narrow"), None, None),
        P(("cluster", "narrow")),
        P(("cluster", "narrow"), None),
        P(("cluster", "narrow")),
    )
    out_specs = (P(("cluster", "narrow"), None), P(("cluster", "narrow"), None))
    return jax.shard_map(
        on_device, mesh=mesh, in_specs=in_specs, out_specs=out_specs, check_vma=False
    )
```

```python
import functools

import jax
import jax.numpy as jnp
from jax import lax
from jax.experimental import pallas as pl
from jax.experimental.pallas import tpu as pltpu
from jax.sharding import PartitionSpec as P

ROOT_HALF = 0.7071067811865476
MIB = 1 << 20
F32 = jnp.float32
BF16 = jnp.bfloat16
VMEM = pl.BlockSpec(memory_space=pltpu.VMEM)
SMEM = pl.BlockSpec(memory_space=pltpu.SMEM)
ANY = pl.BlockSpec(memory_space=pl.ANY)
CHUNKS = 2


def dot(left, right):
    return jnp.dot(left, right, preferred_element_type=F32)


def dot_trans(left, right):
    return lax.dot_general(left, right, (((1,), (1,)), ((), ())), preferred_element_type=F32)


def swapped(array, axis, bit):
    return lax.ppermute(array, axis, [(i, i ^ bit) for i in range(lax.axis_size(axis))])


def left_lanes(shape):
    return lax.broadcasted_iota(jnp.int32, shape, 1) < shape[1] // 2


def turn(values):
    return pltpu.roll(values, values.shape[1] // 2, 1)


def split_pairs(rows, block):
    parts = rows.reshape(-1, 2, block, rows.shape[-1])
    return parts[:, 0].reshape(-1, rows.shape[-1]), parts[:, 1].reshape(-1, rows.shape[-1])


def join_pairs(even, odd, block):
    width = even.shape[-1]
    both = jnp.concatenate([even.reshape(-1, 1, block, width), odd.reshape(-1, 1, block, width)], axis=1)
    return both.reshape(-1, width)


def padded(weight):
    none = jnp.zeros_like(weight)
    return jnp.concatenate([weight, none], axis=0), jnp.concatenate([none, weight], axis=0)


def call(kernel, name, limit, flops, moved, **more):
    return pl.pallas_call(
        kernel,
        compiler_params=pltpu.CompilerParams(vmem_limit_bytes=limit),
        cost_estimate=pl.CostEstimate(flops=flops, bytes_accessed=moved, transcendentals=0),
        name=name,
        **more,
    )


def down_kernel(block, x_ref, wt_ref, pre_ref, trip_ref):
    even, odd = split_pairs(x_ref[...], block)
    left, right = padded(wt_ref[...])
    pre = dot_trans(even, left) + dot_trans(odd, right)
    pre_ref[...] = pre
    trip_ref[...] = (pre * (0.5 * jnp.tanh(0.5 * pre) + 0.5)).astype(BF16)


def down(x, wt, block, steps):
    rows, width = x.shape
    lanes = 2 * wt.shape[0]
    thin = pl.BlockSpec((rows // 2 // steps, lanes), lambda i: (i, 0))
    return call(
        functools.partial(down_kernel, block),
        "down",
        8 * MIB,
        2 * rows * width * lanes,
        2 * rows * width,
        grid=(steps,),
        in_specs=[
            pl.BlockSpec((rows // steps, width), lambda i: (i, 0)),
            pl.BlockSpec(wt.shape, lambda i: (0, 0)),
        ],
        out_specs=[thin] * 2,
        out_shape=[
            jax.ShapeDtypeStruct((rows // 2, lanes), F32),
            jax.ShapeDtypeStruct((rows // 2, lanes), BF16),
        ],
    )(x, wt)


def angle_kernel(block, slots, angle_ref, after_ref, in_ref, out_ref, rows_ref, pair_ref):
    del after_ref
    lanes = 2 * block
    half = block // 2
    mask = left_lanes((half, lanes))
    for at in range(angle_ref.shape[0]):
        wide = angle_ref[at].astype(F32)
        for t in range(half):
            rows_ref[at, t * slots : (t + 1) * slots, :] = wide[:, t * lanes : (t + 1) * lanes]
        for s in range(0, slots, 2):
            first = rows_ref[at, pl.ds(s, half, stride=slots), :]
            second = rows_ref[at, pl.ds(s + 1, half, stride=slots), :]
            pair_ref[at, s // 2, pl.ds(0, half, stride=2), :] = jnp.where(mask, first, turn(second))
            pair_ref[at, s // 2, pl.ds(1, half, stride=2), :] = jnp.where(mask, turn(first), second)
    for at in range(0, angle_ref.shape[0], 2):
        for p in range(slots // 2):
            first, second = pair_ref[at, p], pair_ref[at + 1, p]
            in_ref[at, :, p * lanes : (p + 1) * lanes] = first.astype(BF16)
            in_ref[at + 1, :, p * lanes : (p + 1) * lanes] = second.astype(BF16)
            both = jnp.concatenate([first, second], axis=0)
            out_ref[at // 2, p * lanes : (p + 1) * lanes, :] = both.T.astype(BF16)


def turned_angles(angular, after, block, steps):
    blocks, slots, _ = angular.shape
    per = blocks // steps
    lanes = 2 * block
    return call(
        functools.partial(angle_kernel, block, slots),
        "angles",
        16 * MIB,
        0,
        8 * angular.size * 2,
        grid=(steps,),
        in_specs=[pl.BlockSpec((per, slots, block * block), lambda i: (i, 0, 0)), ANY],
        out_specs=[
            pl.BlockSpec((per, block, slots * block), lambda i: (i, 0, 0)),
            pl.BlockSpec((per // 2, slots * block, lanes), lambda i: (i, 0, 0)),
        ],
        out_shape=[
            jax.ShapeDtypeStruct((blocks, block, slots * block), BF16),
            jax.ShapeDtypeStruct((blocks // 2, slots * block, lanes), BF16),
        ],
        scratch_shapes=[
            pltpu.VMEM((per, slots * block // 2, lanes), F32),
            pltpu.VMEM((per, slots // 2, block, lanes), F32),
        ],
    )(angular, after)


def triplet_kernel(block, slots, pieces, chunks, *refs):
    index_ref, row_ref, place_ref, angle_ref = refs[:4]
    piece_refs = refs[4 : 4 + pieces]
    trip_ref = refs[4 + pieces]
    sent_refs = refs[5 + pieces : 5 + pieces + chunks]
    held_ref = refs[-1]
    packed_rows, lanes = trip_ref.shape
    groups = packed_rows // block
    mask = left_lanes((block, lanes))

    for piece in range(pieces):
        rows = piece_refs[piece][...]
        held_ref[piece * groups : (piece + 1) * groups] = rows.reshape(groups, block, lanes)
        rows = turn(rows.astype(F32)).astype(BF16)
        at = (pieces + piece) * groups
        held_ref[at : at + groups] = rows.reshape(groups, block, lanes)
    held_ref[2 * pieces * groups] = jnp.zeros((block, lanes), BF16)

    def target(q, carry):
        sides = []
        for pair in range(2):
            base = (4 * q + 2 * pair) * slots
            picked = [
                jnp.where(mask, held_ref[index_ref[base + s]], held_ref[index_ref[base + slots + s]])
                for s in range(slots)
            ]
            sides.append(jnp.concatenate(picked, axis=0))
        matrix = angle_ref[pl.ds(4 * q, 4)].reshape(4 * block, slots * block)
        every = dot(matrix, jnp.concatenate(sides, axis=1))
        for pair in range(2):
            part = every[pair * 2 * block : (pair + 1) * 2 * block, pair * lanes : (pair + 1) * lanes]
            total = jnp.where(mask, part[:block], part[block:]).astype(BF16)
            trip_ref[pl.ds(pl.multiple_of((2 * q + pair) * block, block), block), :] = total
        return carry

    lax.fori_loop(0, groups // 2, target, 0, unroll=2)

    place = place_ref[...].T
    turned_half = place >= packed_rows
    spread = []
    wide_mask = left_lanes((2 * block, lanes))
    for m in range(groups):
        rows = trip_ref[m * block : (m + 1) * block, :].astype(F32)
        other = turn(rows)
        both = jnp.concatenate([jnp.where(mask, rows, other), jnp.where(mask, other, rows)], axis=0)
        side = jnp.where(place[:, m : m + 1] < packed_rows, 1.0, 0.0)
        lane_side = jnp.where(wide_mask, 1.0, 0.0)
        spread.append(jnp.where(side == lane_side, both, 0.0).astype(BF16))
    spread = jnp.concatenate(spread, axis=0)
    row = row_ref[...]
    row = jnp.where(row < packed_rows, row, row - packed_rows)
    tile = 4 * block
    for t in range(packed_rows // tile):
        spot = lax.broadcasted_iota(jnp.int32, (tile, 2 * packed_rows), 0) + t * tile
        both = dot((spot == row).astype(F32).astype(BF16), spread).astype(BF16)
        at = t * tile
        per = packed_rows // chunks
        sent_refs[at // per][at % per : at % per + tile, :] = both


def triplet(index, row, place, angles, pieces, block, slots, chunks):
    packed_rows, lanes = pieces[0].shape
    held = packed_rows // block * 2 * len(pieces) + 1
    return call(
        functools.partial(triplet_kernel, block, slots, len(pieces), chunks),
        "triplet",
        12 * MIB + 2 * held * block * lanes,
        2 * packed_rows * slots * block * lanes,
        8 * MIB,
        in_specs=[SMEM] + [VMEM] * (3 + len(pieces)),
        out_specs=[VMEM] * (1 + chunks),
        out_shape=[jax.ShapeDtypeStruct((packed_rows, lanes), BF16)]
        + [jax.ShapeDtypeStruct((packed_rows // chunks, lanes), BF16)] * chunks,
        scratch_shapes=[pltpu.VMEM((held, block, lanes), BF16)],
    )(index, row, place, angles, *pieces)


def gated(half_pre):
    lifted = 1.0 + jnp.tanh(half_pre)
    value = half_pre * lifted
    return value, lifted + value * (2.0 - lifted)


def layer_kernel(block, x_ref, ct_ref, own_ref, far_ref, up_ref, wi_ref, wo_ref, *refs):
    out_ref, grad_ref, near_ref, send_ref = refs[-4:]
    up = up_ref[...] * 0.5
    up2 = jnp.concatenate([up, up], axis=0)
    up_left, up_right = padded(up)
    mask = left_lanes(own_ref.shape)
    none = jnp.zeros(own_ref.shape, BF16)

    def pre_up(ref):
        rows = ref[...]
        return dot(join_pairs(jnp.where(mask, rows, none), jnp.where(mask, none, rows), block), up2)

    own_value, own_slope = gated(pre_up(own_ref))
    far_value, far_slope = gated(pre_up(far_ref))
    hidden = x_ref[...].astype(F32) * ROOT_HALF + (own_value + far_value) * 0.5
    wi, wo = wi_ref[...] * 0.5, wo_ref[...] * 0.5
    in_value, in_slope = gated(dot(hidden.astype(BF16), wi))
    out_value, out_slope = gated(dot(in_value.astype(BF16), wo))
    out_ref[...] = ((hidden + out_value) * ROOT_HALF).astype(BF16)
    scaled = ct_ref[...].astype(F32) * (0.5 * ROOT_HALF)
    grad_out = (scaled * out_slope).astype(BF16)
    grad_in = (dot_trans(grad_out, wo) * in_slope).astype(BF16)
    half_grad = scaled + dot_trans(grad_in, wi)
    grad_ref[...] = (half_grad * (2.0 * ROOT_HALF)).astype(BF16)

    def project(rows):
        even, odd = split_pairs(rows.astype(BF16), block)
        return dot_trans(even, up_left) + dot_trans(odd, up_right)

    near_ref[...] = project(half_grad * own_slope)
    send_ref[...] = project(half_grad * far_slope).astype(BF16)


def layer(x, ct, own, far, up, wi, wo, before, block, steps, chunk, chunks):
    rows, width = x.shape
    lanes = own.shape[1]
    rows_in = rows // chunks // steps
    first = chunk * steps
    whole = lambda array: pl.BlockSpec(array.shape, lambda i: (0, 0))
    wide = pl.BlockSpec((rows_in, width), lambda i: (first + i, 0))
    thin = pl.BlockSpec((rows_in // 2, lanes), lambda i: (first + i, 0))
    part = pl.BlockSpec((rows_in // 2, lanes), lambda i: (i, 0))
    return call(
        functools.partial(layer_kernel, block),
        "layer",
        24 * MIB,
        rows // chunks * width * (8 * width + 8 * lanes),
        rows // chunks * width * 8,
        grid=(steps,),
        in_specs=[wide, wide, thin, part] + [whole(w) for w in (up, wi, wo)] + [ANY] * len(before),
        out_specs=[wide, wide, part, part],
        out_shape=[
            jax.ShapeDtypeStruct((rows, width), BF16),
            jax.ShapeDtypeStruct((rows, width), BF16),
            jax.ShapeDtypeStruct((rows // 2 // chunks, lanes), F32),
            jax.ShapeDtypeStruct((rows // 2 // chunks, lanes), BF16),
        ],
        input_output_aliases={7 + i: i for i in range(len(before))},
    )(x, ct, own, far, up, wi, wo, *before)


def scatter_kernel(block, slots, pieces, chunks, index_ref, place_ref, angle_ref, *refs):
    near_refs, far_refs = refs[:chunks], refs[chunks : 2 * chunks]
    out_refs = refs[2 * chunks : 2 * chunks + pieces]
    total_ref, grad_ref = refs[2 * chunks + pieces :]
    packed_rows, lanes = grad_ref.shape
    groups = packed_rows // block
    mask = left_lanes((block, lanes))
    total_ref[...] = jnp.zeros(total_ref.shape, F32)
    place = place_ref[...].T
    per = packed_rows // chunks
    tile = 2 * block
    wide_mask = left_lanes((tile, lanes))
    lane_side = jnp.where(wide_mask, 1.0, 0.0)
    several = 4
    for start in range(0, groups, several):
        spots, sides = [], []
        for m in range(start, start + several):
            column = place[:, m : m + 1]
            low = column < packed_rows
            spot = lax.broadcasted_iota(jnp.int32, (tile, packed_rows), 1)
            spots.append((spot == jnp.where(low, column, column - packed_rows)).astype(F32).astype(BF16))
            sides.append(jnp.where(low, 1.0, 0.0))
        spots = jnp.concatenate(spots, axis=0)
        got = dot(spots[:, :per], far_refs[0][...])
        for c in range(1, chunks):
            got = got + dot(spots[:, c * per : (c + 1) * per], far_refs[c][...])
        for i, m in enumerate(range(start, start + several)):
            mine = jnp.where(sides[i] == lane_side, got[i * tile : (i + 1) * tile], 0.0)
            mine = mine + turn(mine)
            at = m * block
            near = near_refs[at // per][at % per : at % per + block, :]
            grad_ref[at : at + block, :] = (near + jnp.where(mask, mine[:block], mine[block:])).astype(BF16)
    none = jnp.zeros((block, lanes), BF16)

    def target(m, carry):
        rows = grad_ref[pl.ds(pl.multiple_of(m * block, block), block), :]
        pair = jnp.concatenate([jnp.where(mask, rows, none), jnp.where(mask, none, rows)], axis=0)
        terms = dot(angle_ref[m], pair)
        base = m * (2 * slots)
        for s in range(slots):
            term = terms[s * block : (s + 1) * block]
            total_ref[index_ref[base + s]] += jnp.where(mask, term, 0.0)
            total_ref[index_ref[base + slots + s]] += jnp.where(mask, 0.0, term)
        return carry

    lax.fori_loop(0, groups, target, 0, unroll=4)

    for piece in range(pieces):
        at = piece * groups
        straight = total_ref[at : at + groups].reshape(packed_rows, lanes)
        at += pieces * groups
        crossed = total_ref[at : at + groups].reshape(packed_rows, lanes)
        out_refs[piece][...] = (straight + turn(crossed)).astype(out_refs[piece].dtype)


def scatter(index, place, angles, near, far, types, block, slots):
    chunks = len(near)
    packed_rows, lanes = near[0].shape[0] * chunks, near[0].shape[1]
    pieces = len(types)
    held = 2 * pieces * (packed_rows // block) + 1
    return call(
        functools.partial(scatter_kernel, block, slots, pieces, chunks),
        "scatter",
        16 * MIB + 4 * held * block * lanes,
        2 * packed_rows * slots * block * lanes,
        8 * MIB,
        in_specs=[SMEM] + [VMEM] * (2 + 2 * chunks),
        out_specs=[VMEM] * pieces,
        out_shape=[jax.ShapeDtypeStruct((packed_rows, lanes), kind) for kind in types],
        scratch_shapes=[
            pltpu.VMEM((held, block, lanes), F32),
            pltpu.VMEM((packed_rows, lanes), BF16),
        ],
    )(index, place, angles, *near, *far)


def last_kernel(block, pre_ref, grad_ref, wt_ref, *refs):
    out_ref = refs[-1]
    total = refs[0][...].astype(F32)
    for ref in refs[1:-1]:
        total = total + ref[...].astype(F32)
    _, slope = gated(pre_ref[...] * 0.5)
    grad = (total * (0.5 * slope)).astype(BF16)
    left, right = padded(wt_ref[...])
    both = join_pairs(dot(grad, left), dot(grad, right), block)
    out_ref[...] = (grad_ref[...].astype(F32) + both).astype(BF16)


def last(pre, grad_msg, wt, terms, block, steps):
    rows, width = grad_msg.shape
    lanes = 2 * wt.shape[0]
    wide = pl.BlockSpec((rows // steps, width), lambda i: (i, 0))
    thin = pl.BlockSpec((rows // 2 // steps, lanes), lambda i: (i, 0))
    return call(
        functools.partial(last_kernel, block),
        "last",
        16 * MIB,
        2 * rows * width * lanes,
        4 * rows * width,
        grid=(steps,),
        in_specs=[thin, wide, pl.BlockSpec(wt.shape, lambda i: (0, 0))] + [thin] * len(terms),
        out_specs=wide,
        out_shape=jax.ShapeDtypeStruct((rows, width), BF16),
    )(pre, grad_msg, wt, *terms)


def on_device(
    edge_feats,
    cotangent,
    down_weight,
    up_weight,
    inner_weight,
    outer_weight,
    angular,
    reverse,
    sources,
    counts,
):
    lane_count = lax.axis_size("narrow")
    top_bit = lax.axis_size("cluster") // 2
    me = lax.axis_index("narrow")
    local_blocks, slots = sources.shape
    local_edges = edge_feats.shape[0]
    block = local_edges // local_blocks
    groups = local_blocks // 2
    packed_rows = local_edges // 2
    down_trans = down_weight.T

    live = lax.broadcasted_iota(jnp.int32, sources.shape, 1) < counts[:, None]
    local = sources % (local_blocks * lane_count)
    spot = (local // local_blocks ^ me) * local_blocks + local % local_blocks
    odd = lax.broadcasted_iota(jnp.int32, sources.shape, 0) % 2
    turned = jnp.where(spot % 2 == odd, 0, lane_count * groups)
    index = jnp.where(live, turned + spot // 2, 2 * lane_count * groups).reshape(-1)

    slot = reverse % local_edges
    place = (slot // block % 2) * packed_rows + slot // (2 * block) * block + slot % block
    place_row = place.reshape(1, local_edges)
    place = place.reshape(groups, 2 * block)

    pre_down, trip = down(edge_feats, down_trans, block, 4)
    angle_in, angle_out = turned_angles(angular, trip, block, 4)
    pieces = {0: trip}
    bits = [1 << i for i in range(lane_count.bit_length() - 1)]
    for bit in reversed(bits):
        pieces.update({d ^ bit: swapped(piece, "narrow", bit) for d, piece in pieces.items()})
    pieces = [pieces[d] for d in range(lane_count)]
    trip_own, *trip_sent = triplet(index, place_row, place, angle_in, pieces, block, slots, CHUNKS)
    trip_far = [swapped(part, "cluster", top_bit) for part in trip_sent]
    done, near, far = [], [], []
    for chunk in range(CHUNKS):
        *done, own_part, sent = layer(
            edge_feats,
            cotangent,
            trip_own,
            trip_far[chunk],
            up_weight,
            inner_weight[0],
            outer_weight[0],
            done,
            block,
            2,
            chunk,
            CHUNKS,
        )
        near.append(own_part)
        far.append(swapped(sent, "cluster", top_bit))
    output, grad_msg = done
    types = [BF16 if d % 2 else F32 for d in range(lane_count)]
    parts = dict(enumerate(scatter(index, place, angle_out, near, far, types, block, slots)))
    terms = [parts[0]]
    for bit in bits:
        for d in range(lane_count - bit, -1, -2 * bit):
            got = swapped(parts[d].astype(BF16), "narrow", bit)
            if d == bit:
                terms.append(got)
            else:
                parts[d ^ bit] = parts[d ^ bit] + got.astype(F32)
    grad_x = last(pre_down, grad_msg, down_trans, terms, block, 4)
    return (output, grad_x)


def solution(mesh):
    in_specs = (
        P(("cluster", "narrow"), None),
        P(("cluster", "narrow"), None),
        P(),
        P(),
        P(),
        P(),
        P(("cluster", "narrow"), None, None),
        P(("cluster", "narrow")),
        P(("cluster", "narrow"), None),
        P(("cluster", "narrow")),
    )
    out_specs = (P(("cluster", "narrow"), None), P(("cluster", "narrow"), None))
    return jax.shard_map(
        on_device, mesh=mesh, in_specs=in_specs, out_specs=out_specs, check_vma=False
    )
```

```python
import functools

import jax
import jax.numpy as jnp
from jax import lax
from jax.experimental import pallas as pl
from jax.experimental.pallas import tpu as pltpu
from jax.sharding import PartitionSpec as P

ROOT_HALF = 0.7071067811865476
MIB = 1 << 20
F32 = jnp.float32
BF16 = jnp.bfloat16
VMEM = pl.BlockSpec(memory_space=pltpu.VMEM)
SMEM = pl.BlockSpec(memory_space=pltpu.SMEM)
ANY = pl.BlockSpec(memory_space=pl.ANY)
HBM = pl.BlockSpec(memory_space=pltpu.HBM)


def dot(left, right):
    return jnp.dot(left, right, preferred_element_type=F32)


def dot_trans(left, right):
    return lax.dot_general(left, right, (((1,), (1,)), ((), ())), preferred_element_type=F32)


def swapped(array, axis, bit):
    return lax.ppermute(array, axis, [(i, i ^ bit) for i in range(lax.axis_size(axis))])


def left_lanes(shape):
    return lax.broadcasted_iota(jnp.int32, shape, 1) < shape[1] // 2


def turn(values):
    return pltpu.roll(values, values.shape[1] // 2, 1)


def split_pairs(rows, block):
    parts = rows.reshape(-1, 2, block, rows.shape[-1])
    return parts[:, 0].reshape(-1, rows.shape[-1]), parts[:, 1].reshape(-1, rows.shape[-1])


def join_pairs(even, odd, block):
    width = even.shape[-1]
    both = jnp.concatenate([even.reshape(-1, 1, block, width), odd.reshape(-1, 1, block, width)], axis=1)
    return both.reshape(-1, width)


def padded(weight):
    none = jnp.zeros_like(weight)
    return jnp.concatenate([weight, none], axis=0), jnp.concatenate([none, weight], axis=0)


def call(kernel, name, limit, flops, moved, **more):
    return pl.pallas_call(
        kernel,
        compiler_params=pltpu.CompilerParams(vmem_limit_bytes=limit),
        cost_estimate=pl.CostEstimate(flops=flops, bytes_accessed=moved, transcendentals=0),
        name=name,
        **more,
    )


def down_kernel(block, x_ref, wt_ref, pre_ref, trip_ref):
    left, right = padded(wt_ref[...])
    even, odd = split_pairs(x_ref[...], block)
    pre = dot_trans(even, left) + dot_trans(odd, right)
    pre_ref[...] = pre
    trip_ref[...] = (pre * (0.5 * jnp.tanh(0.5 * pre) + 0.5)).astype(BF16)


def down(x, wt, block):
    rows, width = x.shape
    lanes = 2 * wt.shape[0]
    return call(
        functools.partial(down_kernel, block),
        "down",
        8 * MIB,
        2 * rows * width * lanes,
        2 * rows * width,
        in_specs=[VMEM] * 2,
        out_specs=[VMEM] * 2,
        out_shape=[
            jax.ShapeDtypeStruct((rows // 2, lanes), F32),
            jax.ShapeDtypeStruct((rows // 2, lanes), BF16),
        ],
    )(x, wt)


def ahead_kernel(block, slots, angle_ref, row_ref, *refs):
    in_ref, out_ref, spot_ref, token_ref, rows_ref, pair_ref = refs[-6:]
    lanes = 2 * block
    half = block // 2
    mask = left_lanes((half, lanes))
    token_ref[...] = jnp.zeros(token_ref.shape, BF16)

    def pair(m, carry):
        for k in range(2):
            wide = angle_ref[2 * m + k].astype(F32)
            for t in range(half):
                rows_ref[k, t * slots : (t + 1) * slots, :] = wide[:, t * lanes : (t + 1) * lanes]
            for s in range(0, slots, 2):
                first = rows_ref[k, pl.ds(s, half, stride=slots), :]
                second = rows_ref[k, pl.ds(s + 1, half, stride=slots), :]
                pair_ref[k, s // 2, pl.ds(0, half, stride=2), :] = jnp.where(mask, first, turn(second))
                pair_ref[k, s // 2, pl.ds(1, half, stride=2), :] = jnp.where(mask, turn(first), second)
        for p in range(slots // 2):
            first, second = pair_ref[0, p], pair_ref[1, p]
            in_ref[2 * m, :, p * lanes : (p + 1) * lanes] = first.astype(BF16)
            in_ref[2 * m + 1, :, p * lanes : (p + 1) * lanes] = second.astype(BF16)
            both = jnp.concatenate([first, second], axis=0)
            out_ref[m, p * lanes : (p + 1) * lanes, :] = both.T.astype(BF16)
        return carry

    lax.fori_loop(0, angle_ref.shape[0] // 2, pair, 0, unroll=2)
    row = row_ref[...]
    packed_rows = spot_ref.shape[0]
    row = jnp.where(row < packed_rows, row, row - packed_rows)
    tile = packed_rows // 8
    for start in range(0, packed_rows, tile):
        spot = lax.broadcasted_iota(jnp.int32, (tile, row.shape[1]), 0) + start
        spot_ref[start : start + tile, :] = (spot == row).astype(F32).astype(BF16)


def ahead(angular, row, after, block):
    blocks, slots, _ = angular.shape
    edges = row.shape[1]
    lanes = 2 * block
    return call(
        functools.partial(ahead_kernel, block, slots),
        "ahead",
        4 * MIB,
        0,
        8 * angular.size * 2,
        in_specs=[VMEM, VMEM] + [ANY] * len(after),
        out_specs=[VMEM] * 4,
        out_shape=[
            jax.ShapeDtypeStruct((blocks, block, slots * block), BF16),
            jax.ShapeDtypeStruct((blocks // 2, slots * block, lanes), BF16),
            jax.ShapeDtypeStruct((edges // 2, edges), BF16),
            jax.ShapeDtypeStruct((16, lanes), BF16),
        ],
        scratch_shapes=[
            pltpu.VMEM((2, slots * block // 2, lanes), F32),
            pltpu.VMEM((2, slots // 2, block, lanes), F32),
        ],
    )(angular, row, *after)


def triplet_kernel(block, slots, pieces, parts, *refs):
    index_ref, spot_ref, place_ref, angle_ref = refs[:4]
    piece_refs = refs[4 : 4 + pieces]
    trip_ref = refs[5 + pieces]
    sent_refs = refs[6 + pieces : 6 + pieces + len(parts)]
    held_ref = refs[-1]
    packed_rows, lanes = trip_ref.shape
    groups = packed_rows // block
    mask = left_lanes((block, lanes))

    for piece in range(pieces):
        rows = piece_refs[piece][...]
        held_ref[piece * groups : (piece + 1) * groups] = rows.reshape(groups, block, lanes)
        rows = turn(rows.astype(F32)).astype(BF16)
        at = (pieces + piece) * groups
        held_ref[at : at + groups] = rows.reshape(groups, block, lanes)
    held_ref[2 * pieces * groups] = jnp.zeros((block, lanes), BF16)

    def target(q, carry):
        sides = []
        for pair in range(2):
            base = (4 * q + 2 * pair) * slots
            picked = [
                jnp.where(mask, held_ref[index_ref[base + s]], held_ref[index_ref[base + slots + s]])
                for s in range(slots)
            ]
            sides.append(jnp.concatenate(picked, axis=0))
        matrix = angle_ref[pl.ds(4 * q, 4)].reshape(4 * block, slots * block)
        every = dot(matrix, jnp.concatenate(sides, axis=1))
        for pair in range(2):
            part = every[pair * 2 * block : (pair + 1) * 2 * block, pair * lanes : (pair + 1) * lanes]
            total = jnp.where(mask, part[:block], part[block:]).astype(BF16)
            trip_ref[pl.ds(pl.multiple_of((2 * q + pair) * block, block), block), :] = total
        return carry

    lax.fori_loop(0, groups // 2, target, 0, unroll=2)

    place = place_ref[...].T
    turned_half = place >= packed_rows
    spread = []
    wide_mask = left_lanes((2 * block, lanes))
    for m in range(groups):
        rows = trip_ref[m * block : (m + 1) * block, :].astype(F32)
        other = turn(rows)
        both = jnp.concatenate([jnp.where(mask, rows, other), jnp.where(mask, other, rows)], axis=0)
        side = jnp.where(place[:, m : m + 1] < packed_rows, 1.0, 0.0)
        lane_side = jnp.where(wide_mask, 1.0, 0.0)
        spread.append(jnp.where(side == lane_side, both, 0.0).astype(BF16))
    spread = jnp.concatenate(spread, axis=0)
    first = 0
    for part, sent_ref in zip(parts, sent_refs):
        rows = slice(first * block, (first + part) * block)
        sent_ref[...] = dot(spot_ref[rows, :], spread).astype(BF16)
        first += part


def triplet(index, spot, place, angles, pieces, after, block, slots, parts):
    packed_rows, lanes = pieces[0].shape
    held = packed_rows // block * 2 * len(pieces) + 1
    return call(
        functools.partial(triplet_kernel, block, slots, len(pieces), parts),
        "triplet",
        6 * MIB + 2 * held * block * lanes,
        2 * packed_rows * slots * block * lanes,
        8 * MIB,
        in_specs=[SMEM] + [VMEM] * (3 + len(pieces)) + [ANY],
        out_specs=[VMEM] * (1 + len(parts)),
        out_shape=[jax.ShapeDtypeStruct((packed_rows, lanes), BF16)]
        + [jax.ShapeDtypeStruct((part * block, lanes), BF16) for part in parts],
        scratch_shapes=[pltpu.VMEM((held, block, lanes), BF16)],
    )(index, spot, place, angles, *pieces, after)


def gated(half_pre):
    lifted = 1.0 + jnp.tanh(half_pre)
    value = half_pre * lifted
    return value, lifted + value * (2.0 - lifted)


def pre_up(rows, up, block):
    up2 = jnp.concatenate([up, up], axis=0)
    mask = left_lanes(rows.shape)
    none = jnp.zeros(rows.shape, BF16)
    return dot(join_pairs(jnp.where(mask, rows, none), jnp.where(mask, none, rows), block), up2)


def project(rows, up, block):
    both = dot_trans(rows.astype(BF16), jnp.concatenate([up, up], axis=0))
    even, odd = split_pairs(both, block)
    return jnp.where(left_lanes(even.shape), even, odd)


def gate_kernel(block, tile, x_ref, own_ref, up_ref, base_ref, slope_ref):
    up = up_ref[...] * 0.5
    for start in range(0, x_ref.shape[0], tile):
        rows = own_ref[start // 2 : (start + tile) // 2, :]
        value, slope = gated(pre_up(rows, up, block))
        wide = slice(start, start + tile)
        base_ref[wide, :] = x_ref[wide, :].astype(F32) * ROOT_HALF + value * 0.5
        slope_ref[wide, :] = slope.astype(BF16)


def gate(x, own, up, block):
    rows, width = x.shape
    return call(
        functools.partial(gate_kernel, block, 8 * block),
        "gate",
        8 * MIB,
        2 * rows * width * own.shape[1],
        8 * rows * width,
        in_specs=[VMEM] * 3,
        out_specs=[VMEM] * 2,
        out_shape=[
            jax.ShapeDtypeStruct((rows, width), F32),
            jax.ShapeDtypeStruct((rows, width), BF16),
        ],
    )(x, own, up)


def layer_kernel(block, first, far_first, base_ref, ct_ref, far_ref, up_ref, wi_ref, wo_ref, *refs):
    out_ref, grad_ref, send_ref, held_ref, sem = refs[-5:]
    rows = grad_ref.shape[0]
    wide = slice(first * 2 * block, first * 2 * block + rows)
    up = up_ref[...] * 0.5
    far = far_ref[far_first * block : far_first * block + rows // 2, :]
    far_value, far_slope = gated(pre_up(far, up, block))
    hidden = base_ref[wide, :] + far_value * 0.5
    wi, wo = wi_ref[...] * 0.5, wo_ref[...] * 0.5
    in_value, in_slope = gated(dot(hidden.astype(BF16), wi))
    out_value, out_slope = gated(dot(in_value.astype(BF16), wo))
    held_ref[...] = ((hidden + out_value) * ROOT_HALF).astype(BF16)
    copy = pltpu.make_async_copy(held_ref, out_ref.at[wide, :], sem)
    copy.start()
    scaled = ct_ref[wide, :].astype(F32) * (0.5 * ROOT_HALF)
    grad_out = (scaled * out_slope).astype(BF16)
    grad_in = (dot_trans(grad_out, wo) * in_slope).astype(BF16)
    half_grad = scaled + dot_trans(grad_in, wi)
    grad_ref[...] = (half_grad * (2.0 * ROOT_HALF)).astype(BF16)
    send_ref[...] = project(half_grad * far_slope, up, block).astype(BF16)
    copy.wait()


def layer(base, ct, far, up, wi, wo, before, block, first, part, far_first):
    rows, width = base.shape
    lanes = far.shape[1]
    return call(
        functools.partial(layer_kernel, block, first, far_first),
        "layer",
        32 * MIB,
        0,
        0,
        in_specs=[VMEM] * 6 + [HBM] * len(before),
        out_specs=[HBM, VMEM, VMEM],
        out_shape=[
            jax.ShapeDtypeStruct((rows, width), BF16),
            jax.ShapeDtypeStruct((part * 2 * block, width), BF16),
            jax.ShapeDtypeStruct((part * block, lanes), BF16),
        ],
        scratch_shapes=[pltpu.VMEM((part * 2 * block, width), BF16), pltpu.SemaphoreType.DMA(())],
        input_output_aliases={6 + i: i for i in range(len(before))},
    )(base, ct, far, up, wi, wo, *before)


def near_kernel(block, slope_ref, up_ref, place_ref, *refs):
    near_ref, spot_ref = refs[-2:]
    packed_rows = near_ref.shape[0]
    place = place_ref[...].T
    tile = 2 * block
    for m in range(packed_rows // block):
        column = place[:, m : m + 1]
        column = jnp.where(column < packed_rows, column, column - packed_rows)
        spot = lax.broadcasted_iota(jnp.int32, (tile, packed_rows), 1)
        spot_ref[m * tile : (m + 1) * tile, :] = (spot == column).astype(F32).astype(BF16)
    up = up_ref[...] * 0.5
    first = 0
    for grad_ref in refs[:-2]:
        rows = grad_ref.shape[0]
        both = grad_ref[...].astype(F32) * slope_ref[first : first + rows, :].astype(F32)
        near_ref[first // 2 : (first + rows) // 2, :] = project(both, up, block) * ROOT_HALF
        first += rows


def near_part(slope, up, place, grads, block):
    rows, width = slope.shape
    lanes = 2 * up.shape[0]
    return call(
        functools.partial(near_kernel, block),
        "near",
        8 * MIB,
        2 * rows * width * lanes,
        4 * rows * width,
        in_specs=[VMEM] * (3 + len(grads)),
        out_specs=[VMEM] * 2,
        out_shape=[
            jax.ShapeDtypeStruct((rows // 2, lanes), F32),
            jax.ShapeDtypeStruct((rows, rows // 2), BF16),
        ],
    )(slope, up, place, *grads)


def scatter_kernel(block, slots, pieces, chunks, index_ref, place_ref, spot_ref, angle_ref, near_ref, *refs):
    far_refs = refs[:chunks]
    out_refs = refs[chunks : chunks + pieces]
    total_ref, grad_ref = refs[chunks + pieces :]
    packed_rows, lanes = grad_ref.shape
    groups = packed_rows // block
    mask = left_lanes((block, lanes))
    total_ref[...] = jnp.zeros(total_ref.shape, F32)
    place = place_ref[...].T
    tile = 2 * block
    wide_mask = left_lanes((tile, lanes))
    lane_side = jnp.where(wide_mask, 1.0, 0.0)
    far = jnp.concatenate([far_ref[...] for far_ref in far_refs], axis=0)
    several = 4
    for start in range(0, groups, several):
        got = dot(spot_ref[start * tile : (start + several) * tile, :], far)
        for i, m in enumerate(range(start, start + several)):
            side = jnp.where(place[:, m : m + 1] < packed_rows, 1.0, 0.0)
            mine = jnp.where(side == lane_side, got[i * tile : (i + 1) * tile], 0.0)
            mine = mine + turn(mine)
            at = m * block
            both = near_ref[at : at + block, :] + jnp.where(mask, mine[:block], mine[block:])
            grad_ref[at : at + block, :] = both.astype(BF16)
    none = jnp.zeros((block, lanes), BF16)

    def target(m, carry):
        rows = grad_ref[pl.ds(pl.multiple_of(m * block, block), block), :]
        pair = jnp.concatenate([jnp.where(mask, rows, none), jnp.where(mask, none, rows)], axis=0)
        terms = dot(angle_ref[m], pair)
        base = m * (2 * slots)
        for s in range(slots):
            term = terms[s * block : (s + 1) * block]
            total_ref[index_ref[base + s]] += jnp.where(mask, term, 0.0)
            total_ref[index_ref[base + slots + s]] += jnp.where(mask, 0.0, term)
        return carry

    lax.fori_loop(0, groups, target, 0, unroll=4)

    for piece in range(pieces):
        at = piece * groups
        straight = total_ref[at : at + groups].reshape(packed_rows, lanes)
        at += pieces * groups
        crossed = total_ref[at : at + groups].reshape(packed_rows, lanes)
        out_refs[piece][...] = (straight + turn(crossed)).astype(out_refs[piece].dtype)


def scatter(index, place, spot, angles, near, far, types, block, slots):
    chunks = len(far)
    packed_rows, lanes = near.shape
    pieces = len(types)
    held = 2 * pieces * (packed_rows // block) + 1
    return call(
        functools.partial(scatter_kernel, block, slots, pieces, chunks),
        "scatter",
        16 * MIB + 4 * held * block * lanes,
        2 * packed_rows * slots * block * lanes,
        8 * MIB,
        in_specs=[SMEM] + [VMEM] * (4 + chunks),
        out_specs=[VMEM] * pieces,
        out_shape=[jax.ShapeDtypeStruct((packed_rows, lanes), kind) for kind in types],
        scratch_shapes=[
            pltpu.VMEM((held, block, lanes), F32),
            pltpu.VMEM((packed_rows, lanes), BF16),
        ],
    )(index, place, spot, angles, near, *far)


def last_kernel(block, grads, pre_ref, wt_ref, *refs):
    grad_refs, term_refs = refs[:grads], refs[grads:-3]
    out_ref, held_ref, sems = refs[-3:]
    left, right = padded(wt_ref[...])
    first = 0
    copies = []
    for i, grad_ref in enumerate(grad_refs):
        rows = grad_ref.shape[0]
        thin = slice(first // 2, (first + rows) // 2)
        wide = slice(first, first + rows)
        total = term_refs[0][thin, :].astype(F32)
        for ref in term_refs[1:]:
            total = total + ref[thin, :].astype(F32)
        _, slope = gated(pre_ref[thin, :] * 0.5)
        grad = (total * (0.5 * slope)).astype(BF16)
        both = join_pairs(dot(grad, left), dot(grad, right), block)
        held_ref[wide, :] = (grad_ref[...].astype(F32) + both).astype(BF16)
        copies.append(pltpu.make_async_copy(held_ref.at[wide, :], out_ref.at[wide, :], sems.at[i]))
        copies[-1].start()
        first += rows
    for copy in copies:
        copy.wait()


def last(pre, grads, wt, terms, block):
    rows, width = 2 * pre.shape[0], wt.shape[1]
    return call(
        functools.partial(last_kernel, block, len(grads)),
        "last",
        8 * MIB,
        2 * rows * width * pre.shape[1],
        4 * rows * width,
        in_specs=[VMEM] * (2 + len(grads) + len(terms)),
        out_specs=HBM,
        out_shape=jax.ShapeDtypeStruct((rows, width), BF16),
        scratch_shapes=[pltpu.VMEM((rows, width), BF16), pltpu.SemaphoreType.DMA((len(grads),))],
    )(pre, wt, *grads, *terms)


def on_device(
    edge_feats,
    cotangent,
    down_weight,
    up_weight,
    inner_weight,
    outer_weight,
    angular,
    reverse,
    sources,
    counts,
):
    lane_count = lax.axis_size("narrow")
    top_bit = lax.axis_size("cluster") // 2
    me = lax.axis_index("narrow")
    local_blocks, slots = sources.shape
    local_edges = edge_feats.shape[0]
    block = local_edges // local_blocks
    groups = local_blocks // 2
    packed_rows = local_edges // 2
    down_trans = down_weight.T

    live = lax.broadcasted_iota(jnp.int32, sources.shape, 1) < counts[:, None]
    local = sources % (local_blocks * lane_count)
    spot = (local // local_blocks ^ me) * local_blocks + local % local_blocks
    odd = lax.broadcasted_iota(jnp.int32, sources.shape, 0) % 2
    turned = jnp.where(spot % 2 == odd, 0, lane_count * groups)
    index = jnp.where(live, turned + spot // 2, 2 * lane_count * groups).reshape(-1)

    slot = reverse % local_edges
    place = (slot // block % 2) * packed_rows + slot // (2 * block) * block + slot % block
    place_row = place.reshape(1, local_edges)
    place = place.reshape(groups, 2 * block)

    pre_down, trip = down(edge_feats, down_trans, block)
    angle_in, angle_out, spot, token = ahead(angular, place_row, [trip, index, place], block)
    pieces = {0: trip}
    bits = [1 << i for i in range(lane_count.bit_length() - 1)]
    for bit in reversed(bits):
        if bit == 1:
            last_piece = lane_count - 2
            pieces[last_piece], token = lax.optimization_barrier((pieces[last_piece], token))
        pieces.update({d ^ bit: swapped(piece, "narrow", bit) for d, piece in pieces.items()})
    pieces = [pieces[d] for d in range(lane_count)]
    cuts = [0, groups * 7 // 16, groups * 12 // 16, groups]
    parts = [end - start for start, end in zip(cuts, cuts[1:])]
    sizes = [parts[0], groups - parts[0]]
    trip_own, early, late = triplet(index, spot, place, angle_in, pieces, token, block, slots, sizes)
    early = swapped(early, "cluster", top_bit)
    base, slope = gate(edge_feats, trip_own, up_weight, block)
    early, late = lax.optimization_barrier((early, late))
    late = swapped(late, "cluster", top_bit)
    done, grads, far = [], [], []
    for first, part in zip(cuts, parts):
        output, grad, sent = layer(
            base,
            cotangent,
            late if first else early,
            up_weight,
            inner_weight[0],
            outer_weight[0],
            done,
            block,
            first,
            part,
            first - parts[0] if first else 0,
        )
        done = [output]
        grads.append(grad)
        far.append(swapped(sent, "cluster", top_bit))
    near, spot = near_part(slope, up_weight, place, grads, block)
    types = [BF16 if d % 2 else F32 for d in range(lane_count)]
    sums = dict(enumerate(scatter(index, place, spot, angle_out, near, far, types, block, slots)))
    terms = [sums[0]]
    for bit in bits:
        for d in range(lane_count - bit, -1, -2 * bit):
            got = swapped(sums[d].astype(BF16), "narrow", bit)
            if d == bit:
                terms.append(got)
            else:
                sums[d ^ bit] = sums[d ^ bit] + got.astype(F32)
    grad_x = last(pre_down, grads, down_trans, terms, block)
    return (output, grad_x)


def solution(mesh):
    in_specs = (
        P(("cluster", "narrow"), None),
        P(("cluster", "narrow"), None),
        P(),
        P(),
        P(),
        P(),
        P(("cluster", "narrow"), None, None),
        P(("cluster", "narrow")),
        P(("cluster", "narrow"), None),
        P(("cluster", "narrow")),
    )
    out_specs = (P(("cluster", "narrow"), None), P(("cluster", "narrow"), None))
    return jax.shard_map(
        on_device, mesh=mesh, in_specs=in_specs, out_specs=out_specs, check_vma=False
    )
```

```python
import functools

import jax
import jax.numpy as jnp
from jax import lax
from jax.experimental import pallas as pl
from jax.experimental.pallas import tpu as pltpu
from jax.sharding import PartitionSpec as P

ROOT_HALF = 0.7071067811865476
MIB = 1 << 20
F32 = jnp.float32
BF16 = jnp.bfloat16
VMEM = pl.BlockSpec(memory_space=pltpu.VMEM)
SMEM = pl.BlockSpec(memory_space=pltpu.SMEM)
ANY = pl.BlockSpec(memory_space=pl.ANY)
HBM = pl.BlockSpec(memory_space=pltpu.HBM)


def dot(left, right):
    return jnp.dot(left, right, preferred_element_type=F32)


def dot_trans(left, right):
    return lax.dot_general(left, right, (((1,), (1,)), ((), ())), preferred_element_type=F32)


def swapped(array, axis, bit):
    return lax.ppermute(array, axis, [(i, i ^ bit) for i in range(lax.axis_size(axis))])


def left_lanes(shape):
    return lax.broadcasted_iota(jnp.int32, shape, 1) < shape[1] // 2


def turn(values):
    return pltpu.roll(values, values.shape[1] // 2, 1)


def split_pairs(rows, block):
    parts = rows.reshape(-1, 2, block, rows.shape[-1])
    return parts[:, 0].reshape(-1, rows.shape[-1]), parts[:, 1].reshape(-1, rows.shape[-1])


def join_pairs(even, odd, block):
    width = even.shape[-1]
    both = jnp.concatenate([even.reshape(-1, 1, block, width), odd.reshape(-1, 1, block, width)], axis=1)
    return both.reshape(-1, width)


def padded(weight):
    none = jnp.zeros_like(weight)
    return jnp.concatenate([weight, none], axis=0), jnp.concatenate([none, weight], axis=0)


def call(kernel, name, limit, flops, moved, **more):
    return pl.pallas_call(
        kernel,
        compiler_params=pltpu.CompilerParams(vmem_limit_bytes=limit),
        cost_estimate=pl.CostEstimate(flops=flops, bytes_accessed=moved, transcendentals=0),
        name=name,
        **more,
    )


def down_kernel(block, x_ref, wt_ref, pre_ref, *refs):
    trip_refs, (x_held, wt_held, sems) = refs[:-3], refs[-3:]
    copies = [
        pltpu.make_async_copy(x_ref, x_held, sems.at[0]),
        pltpu.make_async_copy(wt_ref, wt_held, sems.at[1]),
    ]
    for copy in copies:
        copy.start()
    for copy in copies:
        copy.wait()
    pre = project(x_held[...], wt_held[...], block)
    pre_ref[...] = pre
    trip = (pre * (0.5 * jnp.tanh(0.5 * pre) + 0.5)).astype(BF16)
    first = 0
    for trip_ref in trip_refs:
        trip_ref[...] = trip[first : first + trip_ref.shape[0]]
        first += trip_ref.shape[0]


def down(x, wt, block, halves):
    rows, width = x.shape
    lanes = 2 * wt.shape[0]
    return call(
        functools.partial(down_kernel, block),
        "down",
        12 * MIB,
        2 * rows * width * lanes,
        2 * rows * width,
        in_specs=[HBM] * 2,
        out_specs=[VMEM] * (1 + len(halves)),
        out_shape=[jax.ShapeDtypeStruct((rows // 2, lanes), F32)]
        + [jax.ShapeDtypeStruct((half * block, lanes), BF16) for half in halves],
        scratch_shapes=[
            pltpu.VMEM(x.shape, BF16),
            pltpu.VMEM(wt.shape, BF16),
            pltpu.SemaphoreType.DMA((2,)),
        ],
    )(*[pltpu.with_memory_space_constraint(array, pltpu.HBM) for array in (x, wt)])


def ahead_kernel(block, slots, angle_ref, row_ref, *refs):
    in_ref, out_ref, spot_ref, token_ref, rows_ref, pair_ref = refs[-6:]
    lanes = 2 * block
    half = block // 2
    mask = left_lanes((half, lanes))
    token_ref[...] = jnp.zeros(token_ref.shape, BF16)

    def pair(m, carry):
        for k in range(2):
            wide = angle_ref[2 * m + k].astype(F32)
            for t in range(half):
                rows_ref[k, t * slots : (t + 1) * slots, :] = wide[:, t * lanes : (t + 1) * lanes]
            for s in range(0, slots, 2):
                first = rows_ref[k, pl.ds(s, half, stride=slots), :]
                second = rows_ref[k, pl.ds(s + 1, half, stride=slots), :]
                pair_ref[k, s // 2, pl.ds(0, half, stride=2), :] = jnp.where(mask, first, turn(second))
                pair_ref[k, s // 2, pl.ds(1, half, stride=2), :] = jnp.where(mask, turn(first), second)
        for p in range(slots // 2):
            first, second = pair_ref[0, p], pair_ref[1, p]
            in_ref[2 * m, :, p * lanes : (p + 1) * lanes] = first.astype(BF16)
            in_ref[2 * m + 1, :, p * lanes : (p + 1) * lanes] = second.astype(BF16)
            both = jnp.concatenate([first, second], axis=0)
            out_ref[m, p * lanes : (p + 1) * lanes, :] = both.T.astype(BF16)
        return carry

    lax.fori_loop(0, angle_ref.shape[0] // 2, pair, 0, unroll=2)
    row = row_ref[...]
    packed_rows = spot_ref.shape[0]
    row = jnp.where(row < packed_rows, row, row - packed_rows)
    tile = packed_rows // 8
    for start in range(0, packed_rows, tile):
        spot = lax.broadcasted_iota(jnp.int32, (tile, row.shape[1]), 0) + start
        spot_ref[start : start + tile, :] = (spot == row).astype(F32).astype(BF16)


def ahead(angular, row, after, block):
    blocks, slots, _ = angular.shape
    edges = row.shape[1]
    lanes = 2 * block
    return call(
        functools.partial(ahead_kernel, block, slots),
        "ahead",
        20 * MIB,
        0,
        8 * angular.size * 2,
        in_specs=[VMEM, VMEM] + [ANY] * len(after),
        out_specs=[VMEM] * 4,
        out_shape=[
            jax.ShapeDtypeStruct((blocks, block, slots * block), BF16),
            jax.ShapeDtypeStruct((blocks // 2, slots * block, lanes), BF16),
            jax.ShapeDtypeStruct((edges // 2, edges), BF16),
            jax.ShapeDtypeStruct((16, lanes), BF16),
        ],
        scratch_shapes=[
            pltpu.VMEM((2, slots * block // 2, lanes), F32),
            pltpu.VMEM((2, slots // 2, block, lanes), F32),
        ],
    )(angular, row, *after)


def triplet_kernel(block, slots, pieces, halves, parts, *refs):
    index_ref, spot_ref, place_ref, angle_ref = refs[:4]
    piece_refs = refs[4 : 4 + halves * pieces]
    trip_ref = refs[5 + halves * pieces]
    sent_refs = refs[-1 - len(parts) : -1]
    held_ref = refs[-1]
    packed_rows, lanes = trip_ref.shape
    groups = packed_rows // block
    mask = left_lanes((block, lanes))

    at = 0
    for piece_ref in piece_refs:
        rows = piece_ref[...]
        here = rows.shape[0] // block
        held_ref[at : at + here] = rows.reshape(here, block, lanes)
        rows = turn(rows.astype(F32)).astype(BF16)
        held_ref[pieces * groups + at : pieces * groups + at + here] = rows.reshape(here, block, lanes)
        at += here
    held_ref[2 * pieces * groups] = jnp.zeros((block, lanes), BF16)

    def target(q, carry):
        sides = []
        for pair in range(2):
            base = (4 * q + 2 * pair) * slots
            picked = [
                jnp.where(mask, held_ref[index_ref[base + s]], held_ref[index_ref[base + slots + s]])
                for s in range(slots)
            ]
            sides.append(jnp.concatenate(picked, axis=0))
        matrix = angle_ref[pl.ds(4 * q, 4)].reshape(4 * block, slots * block)
        every = dot(matrix, jnp.concatenate(sides, axis=1))
        for pair in range(2):
            part = every[pair * 2 * block : (pair + 1) * 2 * block, pair * lanes : (pair + 1) * lanes]
            total = jnp.where(mask, part[:block], part[block:]).astype(BF16)
            trip_ref[pl.ds(pl.multiple_of((2 * q + pair) * block, block), block), :] = total
        return carry

    lax.fori_loop(0, groups // 2, target, 0, unroll=True)

    place = place_ref[...].T
    turned_half = place >= packed_rows
    spread = []
    wide_mask = left_lanes((2 * block, lanes))
    for m in range(groups):
        rows = trip_ref[m * block : (m + 1) * block, :].astype(F32)
        other = turn(rows)
        both = jnp.concatenate([jnp.where(mask, rows, other), jnp.where(mask, other, rows)], axis=0)
        side = jnp.where(place[:, m : m + 1] < packed_rows, 1.0, 0.0)
        lane_side = jnp.where(wide_mask, 1.0, 0.0)
        spread.append(jnp.where(side == lane_side, both, 0.0).astype(BF16))
    spread = jnp.concatenate(spread, axis=0)
    first = 0
    for part, sent_ref in zip(parts, sent_refs):
        rows = slice(first * block, (first + part) * block)
        sent_ref[...] = dot(spot_ref[rows, :], spread).astype(BF16)
        first += part


def triplet(index, spot, place, angles, pieces, after, block, slots, parts):
    count, halves = len(pieces), len(pieces[0])
    pieces = [half for piece in pieces for half in piece]
    lanes = pieces[0].shape[1]
    packed_rows = sum(half.shape[0] for half in pieces) // count
    held = packed_rows // block * 2 * count + 1
    return call(
        functools.partial(triplet_kernel, block, slots, count, halves, parts),
        "triplet",
        6 * MIB + 2 * held * block * lanes,
        2 * packed_rows * slots * block * lanes,
        8 * MIB,
        in_specs=[SMEM] + [VMEM] * (3 + len(pieces)) + [ANY],
        out_specs=[VMEM] * (1 + len(parts)),
        out_shape=[jax.ShapeDtypeStruct((packed_rows, lanes), BF16)]
        + [jax.ShapeDtypeStruct((part * block, lanes), BF16) for part in parts],
        scratch_shapes=[pltpu.VMEM((held, block, lanes), BF16)],
    )(index, spot, place, angles, *pieces, after)


def gated(half_pre):
    lifted = 1.0 + jnp.tanh(half_pre)
    value = half_pre * lifted
    return value, lifted + value * (2.0 - lifted)


def pre_up(rows, up, block):
    up2 = jnp.concatenate([up, up], axis=0)
    mask = left_lanes(rows.shape)
    none = jnp.zeros(rows.shape, BF16)
    return dot(join_pairs(jnp.where(mask, rows, none), jnp.where(mask, none, rows), block), up2)


def project(rows, up, block):
    both = dot_trans(rows.astype(BF16), jnp.concatenate([up, up], axis=0))
    even, odd = split_pairs(both, block)
    return jnp.where(left_lanes(even.shape), even, odd)


def gate_kernel(block, tile, x_ref, own_ref, up_ref, base_ref, slope_ref):
    up = up_ref[...] * 0.5
    for start in range(0, x_ref.shape[0], tile):
        rows = own_ref[start // 2 : (start + tile) // 2, :]
        value, slope = gated(pre_up(rows, up, block))
        wide = slice(start, start + tile)
        base_ref[wide, :] = x_ref[wide, :].astype(F32) * ROOT_HALF + value * 0.5
        slope_ref[wide, :] = slope.astype(BF16)


def gate(x, own, up, block):
    rows, width = x.shape
    return call(
        functools.partial(gate_kernel, block, 8 * block),
        "gate",
        8 * MIB,
        2 * rows * width * own.shape[1],
        8 * rows * width,
        in_specs=[VMEM] * 3,
        out_specs=[VMEM] * 2,
        out_shape=[
            jax.ShapeDtypeStruct((rows, width), F32),
            jax.ShapeDtypeStruct((rows, width), BF16),
        ],
    )(x, own, up)


def layer_kernel(block, first, far_first, base_ref, ct_ref, far_ref, up_ref, wi_ref, wo_ref, *refs):
    out_ref, grad_ref, send_ref, held_ref, sem = refs[-5:]
    rows = grad_ref.shape[0]
    wide = slice(first * 2 * block, first * 2 * block + rows)
    up = up_ref[...] * 0.5
    far = far_ref[far_first * block : far_first * block + rows // 2, :]
    far_value, far_slope = gated(pre_up(far, up, block))
    hidden = base_ref[wide, :] + far_value * 0.5
    wi, wo = wi_ref[...] * 0.5, wo_ref[...] * 0.5
    in_value, in_slope = gated(dot(hidden.astype(BF16), wi))
    out_value, out_slope = gated(dot(in_value.astype(BF16), wo))
    held_ref[...] = ((hidden + out_value) * ROOT_HALF).astype(BF16)
    copy = pltpu.make_async_copy(held_ref, out_ref.at[wide, :], sem)
    copy.start()
    scaled = ct_ref[wide, :].astype(F32) * (0.5 * ROOT_HALF)
    grad_out = (scaled * out_slope).astype(BF16)
    grad_in = (dot_trans(grad_out, wo) * in_slope).astype(BF16)
    half_grad = scaled + dot_trans(grad_in, wi)
    grad_ref[...] = (half_grad * (2.0 * ROOT_HALF)).astype(BF16)
    send_ref[...] = project(half_grad * far_slope, up, block).astype(BF16)
    copy.wait()


def layer(base, ct, far, up, wi, wo, before, block, first, part, far_first):
    rows, width = base.shape
    lanes = far.shape[1]
    return call(
        functools.partial(layer_kernel, block, first, far_first),
        "layer",
        32 * MIB,
        0,
        0,
        in_specs=[VMEM] * 6 + [HBM] * len(before),
        out_specs=[HBM, VMEM, VMEM],
        out_shape=[
            jax.ShapeDtypeStruct((rows, width), BF16),
            jax.ShapeDtypeStruct((part * 2 * block, width), BF16),
            jax.ShapeDtypeStruct((part * block, lanes), BF16),
        ],
        scratch_shapes=[pltpu.VMEM((part * 2 * block, width), BF16), pltpu.SemaphoreType.DMA(())],
        input_output_aliases={6 + i: i for i in range(len(before))},
    )(base, ct, far, up, wi, wo, *before)


def near_kernel(block, slope_ref, up_ref, place_ref, *refs):
    near_ref, spot_ref = refs[-2:]
    packed_rows = near_ref.shape[0]
    place = place_ref[...].T
    tile = 2 * block
    for m in range(packed_rows // block):
        column = place[:, m : m + 1]
        folded = spot_ref.shape[1]
        spot = lax.broadcasted_iota(jnp.int32, (tile, folded), 1)
        column = lax.rem(column, folded)
        spot_ref[m * tile : (m + 1) * tile, :] = (spot == column).astype(F32).astype(BF16)
    up = up_ref[...] * 0.5
    first = 0
    for grad_ref in refs[:-2]:
        rows = grad_ref.shape[0]
        both = grad_ref[...].astype(F32) * slope_ref[first : first + rows, :].astype(F32)
        near_ref[first // 2 : (first + rows) // 2, :] = project(both, up, block) * ROOT_HALF
        first += rows


def near_part(slope, up, place, grads, block):
    rows, width = slope.shape
    lanes = 2 * up.shape[0]
    return call(
        functools.partial(near_kernel, block),
        "near",
        8 * MIB,
        2 * rows * width * lanes,
        4 * rows * width,
        in_specs=[VMEM] * (3 + len(grads)),
        out_specs=[VMEM] * 2,
        out_shape=[
            jax.ShapeDtypeStruct((rows // 2, lanes), F32),
            jax.ShapeDtypeStruct((rows, rows // 4), BF16),
        ],
    )(slope, up, place, *grads)


def scatter_kernel(block, slots, pieces, chunks, index_ref, place_ref, spot_ref, angle_ref, near_ref, *refs):
    far_refs, out_refs = refs[:chunks], refs[chunks:-2]
    total_ref, grad_ref = refs[-2:]
    packed_rows, lanes = grad_ref.shape
    groups = packed_rows // block
    mask = left_lanes((block, lanes))
    total_ref[...] = jnp.zeros(total_ref.shape, F32)
    place = place_ref[...].T
    tile = 2 * block
    wide_mask = left_lanes((tile, lanes))
    lane_side = jnp.where(wide_mask, 1.0, 0.0)
    far = jnp.concatenate([far_ref[...] for far_ref in far_refs], axis=0)
    folded = packed_rows // 2
    far = jnp.concatenate([far[:folded], far[folded:]], axis=1)
    several = 4
    for start in range(0, groups, several):
        got = dot(spot_ref[start * tile : (start + several) * tile, :], far)
        for i, m in enumerate(range(start, start + several)):
            column = place[:, m : m + 1]
            side = jnp.where(column < packed_rows, 1.0, 0.0)
            column = jnp.where(column < packed_rows, column, column - packed_rows)
            mine = got[i * tile : (i + 1) * tile]
            mine = jnp.where(column < folded, mine[:, :lanes], mine[:, lanes:])
            mine = jnp.where(side == lane_side, mine, 0.0)
            mine = mine + turn(mine)
            at = m * block
            both = near_ref[at : at + block, :] + jnp.where(mask, mine[:block], mine[block:])
            grad_ref[at : at + block, :] = both.astype(BF16)
    none = jnp.zeros((block, lanes), BF16)

    def target(m, carry):
        rows = grad_ref[pl.ds(pl.multiple_of(m * block, block), block), :]
        pair = jnp.concatenate([jnp.where(mask, rows, none), jnp.where(mask, none, rows)], axis=0)
        terms = dot(angle_ref[m], pair)
        base = m * (2 * slots)
        for s in range(slots):
            term = terms[s * block : (s + 1) * block]
            total_ref[index_ref[base + s]] += jnp.where(mask, term, 0.0)
            total_ref[index_ref[base + slots + s]] += jnp.where(mask, 0.0, term)
        return carry

    lax.fori_loop(0, groups, target, 0, unroll=True)

    for piece in range(pieces):
        at = piece * groups
        for half in range(len(out_refs) // pieces):
            out_ref = out_refs[piece * (len(out_refs) // pieces) + half]
            rows = out_ref.shape[0]
            straight = total_ref[at : at + rows // block].reshape(rows, lanes)
            crossed = total_ref[pieces * groups + at : pieces * groups + at + rows // block].reshape(rows, lanes)
            out_ref[...] = (straight + turn(crossed)).astype(out_ref.dtype)
            at += rows // block


def scatter(index, place, spot, angles, near, far, types, halves, block, slots):
    chunks = len(far)
    packed_rows, lanes = near.shape
    pieces = len(types)
    held = 2 * pieces * (packed_rows // block) + 1
    outs = [jax.ShapeDtypeStruct((half * block, lanes), kind) for kind in types for half in halves]
    return call(
        functools.partial(scatter_kernel, block, slots, pieces, chunks),
        "scatter",
        16 * MIB + 4 * held * block * lanes,
        2 * packed_rows * slots * block * lanes,
        8 * MIB,
        in_specs=[SMEM] + [VMEM] * (4 + chunks),
        out_specs=[VMEM] * len(outs),
        out_shape=outs,
        scratch_shapes=[
            pltpu.VMEM((held, block, lanes), F32),
            pltpu.VMEM((packed_rows, lanes), BF16),
        ],
    )(index, place, spot, angles, near, *far)


def last_kernel(block, grads, terms, start, pre_ref, wt_ref, *refs):
    grad_refs, term_refs = refs[:grads], refs[grads : grads + terms]
    out_ref, held_ref, sem = refs[-3:]
    rows = held_ref.shape[0]
    thin = slice(start // 2, (start + rows) // 2)
    left, right = padded(wt_ref[...])
    total = term_refs[0][...].astype(F32)
    for ref in term_refs[1:]:
        total = total + ref[...].astype(F32)
    _, slope = gated(pre_ref[thin, :] * 0.5)
    grad = (total * (0.5 * slope)).astype(BF16)
    both = join_pairs(dot(grad, left), dot(grad, right), block)
    first = 0
    for grad_ref in grad_refs:
        here = slice(first, first + grad_ref.shape[0])
        held_ref[here, :] = (grad_ref[...].astype(F32) + both[here]).astype(BF16)
        first += grad_ref.shape[0]
    copy = pltpu.make_async_copy(held_ref, out_ref.at[start : start + rows, :], sem)
    copy.start()
    copy.wait()


def last(pre, grads, wt, terms, before, block, start):
    rows, width = 2 * pre.shape[0], wt.shape[1]
    here = 2 * terms[0].shape[0]
    inputs = [pre, wt, *grads, *terms]
    return call(
        functools.partial(last_kernel, block, len(grads), len(terms), start),
        "last",
        12 * MIB,
        0,
        0,
        in_specs=[VMEM] * len(inputs) + [HBM] * len(before),
        out_specs=HBM,
        out_shape=jax.ShapeDtypeStruct((rows, width), BF16),
        scratch_shapes=[pltpu.VMEM((here, width), BF16), pltpu.SemaphoreType.DMA(())],
        input_output_aliases={len(inputs): 0} if before else {},
    )(*inputs, *before)


def on_device(
    edge_feats,
    cotangent,
    down_weight,
    up_weight,
    inner_weight,
    outer_weight,
    angular,
    reverse,
    sources,
    counts,
):
    lane_count = lax.axis_size("narrow")
    top_bit = lax.axis_size("cluster") // 2
    me = lax.axis_index("narrow")
    local_blocks, slots = sources.shape
    local_edges = edge_feats.shape[0]
    block = local_edges // local_blocks
    groups = local_blocks // 2
    packed_rows = local_edges // 2
    down_trans = down_weight.T

    live = lax.broadcasted_iota(jnp.int32, sources.shape, 1) < counts[:, None]
    local = sources % (local_blocks * lane_count)
    spot = (local // local_blocks ^ me) * local_blocks + local % local_blocks
    odd = lax.broadcasted_iota(jnp.int32, sources.shape, 0) % 2
    turned = jnp.where(spot % 2 == odd, 0, lane_count * groups)
    index = jnp.where(live, turned + spot // 2, 2 * lane_count * groups).reshape(-1)

    slot = reverse % local_edges
    place = (slot // block % 2) * packed_rows + slot // (2 * block) * block + slot % block
    place_row = place.reshape(1, local_edges)
    place = place.reshape(groups, 2 * block)

    cuts = [0, groups * 8 // 16, groups * 13 // 16, groups]
    parts = [end - start for start, end in zip(cuts, cuts[1:])]
    sizes = [parts[0], groups - parts[0]]

    pre_down, *trip = down(edge_feats, down_trans, block, [groups])
    angle_in, angle_out, spot, token = ahead(angular, place_row, [trip[0], index, place], block)
    pieces = {0: trip}
    bits = [1 << i for i in range(lane_count.bit_length() - 1)]
    for bit in reversed(bits):
        if bit > 1:
            pieces.update({d ^ bit: [swapped(half, "narrow", bit) for half in piece] for d, piece in pieces.items()})
    more = {d ^ 1: [swapped(half, "narrow", 1) for half in piece] for d, piece in pieces.items() if d + 2 < lane_count}
    here, gone = pieces[lane_count - 2], []
    for i in range(len(here)):
        here[i], token, *gone = lax.optimization_barrier((here[i], token, *gone))
        gone.append(swapped(here[i], "narrow", 1))
    pieces.update(more)
    pieces[lane_count - 1] = gone
    pieces = [pieces[d] for d in range(lane_count)]
    trip_own, early, late = triplet(index, spot, place, angle_in, pieces, token, block, slots, sizes)
    early = swapped(early, "cluster", top_bit)
    base, slope = gate(edge_feats, trip_own, up_weight, block)
    early, late, base, slope = lax.optimization_barrier((early, late, base, slope))
    late = swapped(late, "cluster", top_bit)
    done, grads, far = [], [], []
    for first, part in zip(cuts, parts):
        output, grad, sent = layer(
            base,
            cotangent,
            late if first else early,
            up_weight,
            inner_weight[0],
            outer_weight[0],
            done,
            block,
            first,
            part,
            first - parts[0] if first else 0,
        )
        done = [output]
        grads.append(grad)
        far.append(swapped(sent, "cluster", top_bit))
    near, spot = near_part(slope, up_weight, place, grads, block)
    types = [BF16 if d % 2 else F32 for d in range(lane_count)]
    sums = scatter(index, place, spot, angle_out, near, far, types, sizes, block, slots)
    sums = {d: sums[len(sizes) * d : len(sizes) * (d + 1)] for d in range(lane_count)}
    terms = [[half] for half in sums[0]]
    for bit in bits:
        for d in range(lane_count - bit, -1, -2 * bit):
            got = [swapped(half.astype(BF16), "narrow", bit) for half in sums[d]]
            if d == bit:
                terms = [term + [half] for term, half in zip(terms, got)]
            else:
                sums[d ^ bit] = [held + half.astype(F32) for held, half in zip(sums[d ^ bit], got)]
    grad_x = last(pre_down, grads[:1], down_trans, terms[0], [], block, 0)
    grad_x = last(pre_down, grads[1:], down_trans, terms[1], [grad_x], block, 2 * sizes[0] * block)
    return (output, grad_x)


def solution(mesh):
    in_specs = (
        P(("cluster", "narrow"), None),
        P(("cluster", "narrow"), None),
        P(),
        P(),
        P(),
        P(),
        P(("cluster", "narrow"), None, None),
        P(("cluster", "narrow")),
        P(("cluster", "narrow"), None),
        P(("cluster", "narrow")),
    )
    out_specs = (P(("cluster", "narrow"), None), P(("cluster", "narrow"), None))
    return jax.shard_map(
        on_device, mesh=mesh, in_specs=in_specs, out_specs=out_specs, check_vma=False
    )
```

```python
import functools

import jax
import jax.numpy as jnp
from jax import lax
from jax.experimental import pallas as pl
from jax.experimental.pallas import tpu as pltpu
from jax.sharding import PartitionSpec as P

ROOT_HALF = 0.7071067811865476
MIB = 1 << 20
F32 = jnp.float32
BF16 = jnp.bfloat16
VMEM = pl.BlockSpec(memory_space=pltpu.VMEM)
SMEM = pl.BlockSpec(memory_space=pltpu.SMEM)
ANY = pl.BlockSpec(memory_space=pl.ANY)
HBM = pl.BlockSpec(memory_space=pltpu.HBM)


def dot(left, right):
    return jnp.dot(left, right, preferred_element_type=F32)


def dot_trans(left, right):
    return lax.dot_general(left, right, (((1,), (1,)), ((), ())), preferred_element_type=F32)


def swapped(array, axis, bit):
    return lax.ppermute(array, axis, [(i, i ^ bit) for i in range(lax.axis_size(axis))])


def left_lanes(shape):
    return lax.broadcasted_iota(jnp.int32, shape, 1) < shape[1] // 2


def turn(values):
    return pltpu.roll(values, values.shape[1] // 2, 1)


def split_pairs(rows, block):
    parts = rows.reshape(-1, 2, block, rows.shape[-1])
    return parts[:, 0].reshape(-1, rows.shape[-1]), parts[:, 1].reshape(-1, rows.shape[-1])


def join_pairs(even, odd, block):
    width = even.shape[-1]
    both = jnp.concatenate([even.reshape(-1, 1, block, width), odd.reshape(-1, 1, block, width)], axis=1)
    return both.reshape(-1, width)


def padded(weight):
    none = jnp.zeros_like(weight)
    return jnp.concatenate([weight, none], axis=0), jnp.concatenate([none, weight], axis=0)


def call(kernel, name, limit, flops, moved, **more):
    return pl.pallas_call(
        kernel,
        compiler_params=pltpu.CompilerParams(vmem_limit_bytes=limit),
        cost_estimate=pl.CostEstimate(flops=flops, bytes_accessed=moved, transcendentals=0),
        name=name,
        **more,
    )


def down_kernel(block, x_ref, wt_ref, pre_ref, *refs):
    trip_refs, (x_held, wt_held, sems) = refs[:-3], refs[-3:]
    copies = [
        pltpu.make_async_copy(x_ref, x_held, sems.at[0]),
        pltpu.make_async_copy(wt_ref, wt_held, sems.at[1]),
    ]
    for copy in copies:
        copy.start()
    for copy in copies:
        copy.wait()
    pre = project(x_held[...], wt_held[...], block)
    pre_ref[...] = pre
    trip = (pre * (0.5 * jnp.tanh(0.5 * pre) + 0.5)).astype(BF16)
    first = 0
    for trip_ref in trip_refs:
        trip_ref[...] = trip[first : first + trip_ref.shape[0]]
        first += trip_ref.shape[0]


def down(x, wt, block, halves):
    rows, width = x.shape
    lanes = 2 * wt.shape[0]
    return call(
        functools.partial(down_kernel, block),
        "down",
        12 * MIB,
        2 * rows * width * lanes,
        2 * rows * width,
        in_specs=[HBM] * 2,
        out_specs=[VMEM] * (1 + len(halves)),
        out_shape=[jax.ShapeDtypeStruct((rows // 2, lanes), F32)]
        + [jax.ShapeDtypeStruct((half * block, lanes), BF16) for half in halves],
        scratch_shapes=[
            pltpu.VMEM(x.shape, BF16),
            pltpu.VMEM(wt.shape, BF16),
            pltpu.SemaphoreType.DMA((2,)),
        ],
    )(*[pltpu.with_memory_space_constraint(array, pltpu.HBM) for array in (x, wt)])


def ahead_kernel(block, slots, angle_ref, row_ref, *refs):
    in_ref, out_ref, spot_ref, token_ref, rows_ref, pair_ref = refs[-6:]
    lanes = 2 * block
    half = block // 2
    mask = left_lanes((half, lanes))
    token_ref[...] = jnp.zeros(token_ref.shape, BF16)

    def pair(m, carry):
        for k in range(2):
            wide = angle_ref[2 * m + k].astype(F32)
            for t in range(half):
                rows_ref[k, t * slots : (t + 1) * slots, :] = wide[:, t * lanes : (t + 1) * lanes]
            for s in range(0, slots, 2):
                first = rows_ref[k, pl.ds(s, half, stride=slots), :]
                second = rows_ref[k, pl.ds(s + 1, half, stride=slots), :]
                pair_ref[k, s // 2, pl.ds(0, half, stride=2), :] = jnp.where(mask, first, turn(second))
                pair_ref[k, s // 2, pl.ds(1, half, stride=2), :] = jnp.where(mask, turn(first), second)
        for p in range(slots // 2):
            first, second = pair_ref[0, p], pair_ref[1, p]
            in_ref[2 * m, :, p * lanes : (p + 1) * lanes] = first.astype(BF16)
            in_ref[2 * m + 1, :, p * lanes : (p + 1) * lanes] = second.astype(BF16)
            both = jnp.concatenate([first, second], axis=0)
            out_ref[m, p * lanes : (p + 1) * lanes, :] = both.T.astype(BF16)
        return carry

    lax.fori_loop(0, angle_ref.shape[0] // 2, pair, 0, unroll=2)
    folded = spot_ref.shape[0]
    row = lax.rem(row_ref[...], folded)
    tile = folded // 4
    for start in range(0, folded, tile):
        spot = lax.broadcasted_iota(jnp.int32, (tile, row.shape[1]), 0) + start
        spot_ref[start : start + tile, :] = (spot == row).astype(F32).astype(BF16)


def ahead(angular, row, after, block):
    blocks, slots, _ = angular.shape
    edges = row.shape[1]
    lanes = 2 * block
    return call(
        functools.partial(ahead_kernel, block, slots),
        "ahead",
        20 * MIB,
        0,
        8 * angular.size * 2,
        in_specs=[VMEM, VMEM] + [ANY] * len(after),
        out_specs=[VMEM] * 4,
        out_shape=[
            jax.ShapeDtypeStruct((blocks, block, slots * block), BF16),
            jax.ShapeDtypeStruct((blocks // 2, slots * block, lanes), BF16),
            jax.ShapeDtypeStruct((edges // 4, edges), BF16),
            jax.ShapeDtypeStruct((16, lanes), BF16),
        ],
        scratch_shapes=[
            pltpu.VMEM((2, slots * block // 2, lanes), F32),
            pltpu.VMEM((2, slots // 2, block, lanes), F32),
        ],
    )(angular, row, *after)


def triplet_kernel(block, slots, pieces, halves, parts, *refs):
    index_ref, spot_ref, place_ref, angle_ref = refs[:4]
    piece_refs = refs[4 : 4 + halves * pieces]
    trip_ref = refs[5 + halves * pieces]
    sent_refs = refs[-1 - len(parts) : -1]
    held_ref = refs[-1]
    packed_rows, lanes = trip_ref.shape
    groups = packed_rows // block
    mask = left_lanes((block, lanes))

    at = 0
    for piece_ref in piece_refs:
        rows = piece_ref[...]
        here = rows.shape[0] // block
        held_ref[at : at + here] = rows.reshape(here, block, lanes)
        rows = turn(rows.astype(F32)).astype(BF16)
        held_ref[pieces * groups + at : pieces * groups + at + here] = rows.reshape(here, block, lanes)
        at += here
    held_ref[2 * pieces * groups] = jnp.zeros((block, lanes), BF16)

    def target(q, carry):
        sides = []
        for pair in range(2):
            base = (4 * q + 2 * pair) * slots
            picked = [
                jnp.where(mask, held_ref[index_ref[base + s]], held_ref[index_ref[base + slots + s]])
                for s in range(slots)
            ]
            sides.append(jnp.concatenate(picked, axis=0))
        matrix = angle_ref[pl.ds(4 * q, 4)].reshape(4 * block, slots * block)
        every = dot(matrix, jnp.concatenate(sides, axis=1))
        for pair in range(2):
            part = every[pair * 2 * block : (pair + 1) * 2 * block, pair * lanes : (pair + 1) * lanes]
            total = jnp.where(mask, part[:block], part[block:]).astype(BF16)
            trip_ref[pl.ds(pl.multiple_of((2 * q + pair) * block, block), block), :] = total
        return carry

    lax.fori_loop(0, groups // 2, target, 0, unroll=True)

    place = place_ref[...].T
    folded = packed_rows // 2
    spread = []
    wide_mask = left_lanes((2 * block, lanes))
    lane_side = jnp.where(wide_mask, 1.0, 0.0)
    for m in range(groups):
        rows = trip_ref[m * block : (m + 1) * block, :].astype(F32)
        other = turn(rows)
        both = jnp.concatenate([jnp.where(mask, rows, other), jnp.where(mask, other, rows)], axis=0)
        column = place[:, m : m + 1]
        side = jnp.where(column < packed_rows, 1.0, 0.0)
        column = jnp.where(column < packed_rows, column, column - packed_rows)
        both = jnp.where(side == lane_side, both, 0.0)
        sides = [jnp.where(column < folded, both, 0.0), jnp.where(column < folded, 0.0, both)]
        spread.append(jnp.concatenate(sides, axis=1).astype(BF16))
    sent = dot(spot_ref[...], jnp.concatenate(spread, axis=0)).astype(BF16)
    sent = jnp.concatenate([sent[:, :lanes], sent[:, lanes:]], axis=0)
    first = 0
    for sent_ref in sent_refs:
        sent_ref[...] = sent[first : first + sent_ref.shape[0]]
        first += sent_ref.shape[0]


def triplet(index, spot, place, angles, pieces, after, block, slots, parts):
    count, halves = len(pieces), len(pieces[0])
    pieces = [half for piece in pieces for half in piece]
    lanes = pieces[0].shape[1]
    packed_rows = sum(half.shape[0] for half in pieces) // count
    held = packed_rows // block * 2 * count + 1
    return call(
        functools.partial(triplet_kernel, block, slots, count, halves, parts),
        "triplet",
        6 * MIB + 2 * held * block * lanes,
        2 * packed_rows * slots * block * lanes,
        8 * MIB,
        in_specs=[SMEM] + [VMEM] * (3 + len(pieces)) + [ANY],
        out_specs=[VMEM] * (1 + len(parts)),
        out_shape=[jax.ShapeDtypeStruct((packed_rows, lanes), BF16)]
        + [jax.ShapeDtypeStruct((part * block, lanes), BF16) for part in parts],
        scratch_shapes=[pltpu.VMEM((held, block, lanes), BF16)],
    )(index, spot, place, angles, *pieces, after)


def gated(half_pre):
    lifted = 1.0 + jnp.tanh(half_pre)
    value = half_pre * lifted
    return value, lifted + value * (2.0 - lifted)


def pre_up(rows, up, block):
    up2 = jnp.concatenate([up, up], axis=0)
    mask = left_lanes(rows.shape)
    none = jnp.zeros(rows.shape, BF16)
    return dot(join_pairs(jnp.where(mask, rows, none), jnp.where(mask, none, rows), block), up2)


def project(rows, up, block):
    both = dot_trans(rows.astype(BF16), jnp.concatenate([up, up], axis=0))
    even, odd = split_pairs(both, block)
    return jnp.where(left_lanes(even.shape), even, odd)


def gate_kernel(block, tile, x_ref, own_ref, up_ref, wi_ref, wo_ref, base_ref, slope_ref, wi_half_ref, wo_half_ref):
    up = up_ref[...] * 0.5
    wi_half_ref[...] = wi_ref[...] * 0.5
    wo_half_ref[...] = wo_ref[...] * 0.5
    for start in range(0, x_ref.shape[0], tile):
        rows = own_ref[start // 2 : (start + tile) // 2, :]
        value, slope = gated(pre_up(rows, up, block))
        wide = slice(start, start + tile)
        base_ref[wide, :] = x_ref[wide, :].astype(F32) * ROOT_HALF + value * 0.5
        slope_ref[wide, :] = slope.astype(BF16)


def gate(x, own, up, wi, wo, block):
    rows, width = x.shape
    return call(
        functools.partial(gate_kernel, block, 8 * block),
        "gate",
        8 * MIB,
        2 * rows * width * own.shape[1],
        8 * rows * width,
        in_specs=[VMEM] * 5,
        out_specs=[VMEM] * 4,
        out_shape=[
            jax.ShapeDtypeStruct((rows, width), F32),
            jax.ShapeDtypeStruct((rows, width), BF16),
            jax.ShapeDtypeStruct(wi.shape, BF16),
            jax.ShapeDtypeStruct(wo.shape, BF16),
        ],
    )(x, own, up, wi, wo)


def layer_kernel(block, first, far_first, base_ref, ct_ref, far_ref, up_ref, wi_ref, wo_ref, *refs):
    out_ref, grad_ref, send_ref, held_ref, sem = refs[-5:]
    rows = grad_ref.shape[0]
    wide = slice(first * 2 * block, first * 2 * block + rows)
    up = up_ref[...] * 0.5
    far = far_ref[far_first * block : far_first * block + rows // 2, :]
    far_value, far_slope = gated(pre_up(far, up, block))
    hidden = base_ref[wide, :] + far_value * 0.5
    wi, wo = wi_ref[...], wo_ref[...]
    in_value, in_slope = gated(dot(hidden.astype(BF16), wi))
    out_value, out_slope = gated(dot(in_value.astype(BF16), wo))
    held_ref[...] = ((hidden + out_value) * ROOT_HALF).astype(BF16)
    copy = pltpu.make_async_copy(held_ref, out_ref.at[wide, :], sem)
    copy.start()
    scaled = ct_ref[wide, :].astype(F32) * (0.5 * ROOT_HALF)
    grad_out = (scaled * out_slope).astype(BF16)
    grad_in = (dot_trans(grad_out, wo) * in_slope).astype(BF16)
    half_grad = scaled + dot_trans(grad_in, wi)
    grad_ref[...] = (half_grad * (2.0 * ROOT_HALF)).astype(BF16)
    send_ref[...] = project(half_grad * far_slope, up, block).astype(BF16)
    copy.wait()


def layer(base, ct, far, up, wi, wo, before, block, first, part, far_first):
    rows, width = base.shape
    lanes = far.shape[1]
    return call(
        functools.partial(layer_kernel, block, first, far_first),
        "layer",
        32 * MIB,
        0,
        0,
        in_specs=[VMEM] * 6 + [HBM] * len(before),
        out_specs=[HBM, VMEM, VMEM],
        out_shape=[
            jax.ShapeDtypeStruct((rows, width), BF16),
            jax.ShapeDtypeStruct((part * 2 * block, width), BF16),
            jax.ShapeDtypeStruct((part * block, lanes), BF16),
        ],
        scratch_shapes=[pltpu.VMEM((part * 2 * block, width), BF16), pltpu.SemaphoreType.DMA(())],
        input_output_aliases={6 + i: i for i in range(len(before))},
    )(base, ct, far, up, wi, wo, *before)


def near_kernel(block, slope_ref, up_ref, place_ref, *refs):
    near_ref, spot_ref = refs[-2:]
    packed_rows = near_ref.shape[0]
    place = place_ref[...].T
    tile = 2 * block
    for m in range(packed_rows // block):
        column = place[:, m : m + 1]
        folded = spot_ref.shape[1]
        spot = lax.broadcasted_iota(jnp.int32, (tile, folded), 1)
        column = lax.rem(column, folded)
        spot_ref[m * tile : (m + 1) * tile, :] = (spot == column).astype(F32).astype(BF16)
    up = up_ref[...] * 0.5
    first = 0
    for grad_ref in refs[:-2]:
        rows = grad_ref.shape[0]
        both = grad_ref[...].astype(F32) * slope_ref[first : first + rows, :].astype(F32)
        near_ref[first // 2 : (first + rows) // 2, :] = project(both, up, block) * ROOT_HALF
        first += rows


def near_part(slope, up, place, grads, block):
    rows, width = slope.shape
    lanes = 2 * up.shape[0]
    return call(
        functools.partial(near_kernel, block),
        "near",
        8 * MIB,
        2 * rows * width * lanes,
        4 * rows * width,
        in_specs=[VMEM] * (3 + len(grads)),
        out_specs=[VMEM] * 2,
        out_shape=[
            jax.ShapeDtypeStruct((rows // 2, lanes), F32),
            jax.ShapeDtypeStruct((rows, rows // 4), BF16),
        ],
    )(slope, up, place, *grads)


def scatter_kernel(block, slots, pieces, chunks, index_ref, place_ref, spot_ref, angle_ref, near_ref, *refs):
    far_refs, out_refs = refs[:chunks], refs[chunks:-2]
    total_ref, grad_ref = refs[-2:]
    packed_rows, lanes = grad_ref.shape
    groups = packed_rows // block
    mask = left_lanes((block, lanes))
    total_ref[...] = jnp.zeros(total_ref.shape, F32)
    place = place_ref[...].T
    tile = 2 * block
    wide_mask = left_lanes((tile, lanes))
    lane_side = jnp.where(wide_mask, 1.0, 0.0)
    far = jnp.concatenate([far_ref[...] for far_ref in far_refs], axis=0)
    folded = packed_rows // 2
    far = jnp.concatenate([far[:folded], far[folded:]], axis=1)
    several = 4
    for start in range(0, groups, several):
        got = dot(spot_ref[start * tile : (start + several) * tile, :], far)
        for i, m in enumerate(range(start, start + several)):
            column = place[:, m : m + 1]
            side = jnp.where(column < packed_rows, 1.0, 0.0)
            column = jnp.where(column < packed_rows, column, column - packed_rows)
            mine = got[i * tile : (i + 1) * tile]
            mine = jnp.where(column < folded, mine[:, :lanes], mine[:, lanes:])
            mine = jnp.where(side == lane_side, mine, 0.0)
            mine = mine + turn(mine)
            at = m * block
            both = near_ref[at : at + block, :] + jnp.where(mask, mine[:block], mine[block:])
            grad_ref[at : at + block, :] = both.astype(BF16)
    none = jnp.zeros((block, lanes), BF16)

    def target(q, carry):
        sides = []
        for m in range(2):
            rows = grad_ref[pl.ds(pl.multiple_of((2 * q + m) * block, block), block), :]
            pair = jnp.concatenate([jnp.where(mask, rows, none), jnp.where(mask, none, rows)], axis=0)
            sides.append(jnp.concatenate([jnp.zeros_like(pair)] * m + [pair] + [jnp.zeros_like(pair)] * (1 - m), axis=1))
        matrix = jnp.concatenate([angle_ref[2 * q], angle_ref[2 * q + 1]], axis=1)
        every = dot(matrix, jnp.concatenate(sides, axis=0))
        for m in range(2):
            base = (2 * q + m) * (2 * slots)
            for s in range(slots):
                term = every[s * block : (s + 1) * block, m * lanes : (m + 1) * lanes]
                total_ref[index_ref[base + s]] += jnp.where(mask, term, 0.0)
                total_ref[index_ref[base + slots + s]] += jnp.where(mask, 0.0, term)
        return carry

    lax.fori_loop(0, groups // 2, target, 0, unroll=True)

    for piece in range(pieces):
        at = piece * groups
        for half in range(len(out_refs) // pieces):
            out_ref = out_refs[piece * (len(out_refs) // pieces) + half]
            rows = out_ref.shape[0]
            straight = total_ref[at : at + rows // block].reshape(rows, lanes)
            crossed = total_ref[pieces * groups + at : pieces * groups + at + rows // block].reshape(rows, lanes)
            out_ref[...] = (straight + turn(crossed)).astype(out_ref.dtype)
            at += rows // block


def scatter(index, place, spot, angles, near, far, types, halves, block, slots):
    chunks = len(far)
    packed_rows, lanes = near.shape
    pieces = len(types)
    held = 2 * pieces * (packed_rows // block) + 1
    outs = [jax.ShapeDtypeStruct((half * block, lanes), kind) for kind in types for half in halves]
    return call(
        functools.partial(scatter_kernel, block, slots, pieces, chunks),
        "scatter",
        16 * MIB + 4 * held * block * lanes,
        2 * packed_rows * slots * block * lanes,
        8 * MIB,
        in_specs=[SMEM] + [VMEM] * (4 + chunks),
        out_specs=[VMEM] * len(outs),
        out_shape=outs,
        scratch_shapes=[
            pltpu.VMEM((held, block, lanes), F32),
            pltpu.VMEM((packed_rows, lanes), BF16),
        ],
    )(index, place, spot, angles, near, *far)


def last_kernel(block, grads, terms, start, pre_ref, wt_ref, *refs):
    grad_refs, term_refs = refs[:grads], refs[grads : grads + terms]
    out_ref, held_ref, sem = refs[-3:]
    rows = held_ref.shape[0]
    thin = slice(start // 2, (start + rows) // 2)
    left, right = padded(wt_ref[...])
    total = term_refs[0][...].astype(F32)
    for ref in term_refs[1:]:
        total = total + ref[...].astype(F32)
    _, slope = gated(pre_ref[thin, :] * 0.5)
    grad = (total * (0.5 * slope)).astype(BF16)
    both = join_pairs(dot(grad, left), dot(grad, right), block)
    first = 0
    for grad_ref in grad_refs:
        here = slice(first, first + grad_ref.shape[0])
        held_ref[here, :] = (grad_ref[...].astype(F32) + both[here]).astype(BF16)
        first += grad_ref.shape[0]
    copy = pltpu.make_async_copy(held_ref, out_ref.at[start : start + rows, :], sem)
    copy.start()
    copy.wait()


def last(pre, grads, wt, terms, before, block, start):
    rows, width = 2 * pre.shape[0], wt.shape[1]
    here = 2 * terms[0].shape[0]
    inputs = [pre, wt, *grads, *terms]
    return call(
        functools.partial(last_kernel, block, len(grads), len(terms), start),
        "last",
        12 * MIB,
        0,
        0,
        in_specs=[VMEM] * len(inputs) + [HBM] * len(before),
        out_specs=HBM,
        out_shape=jax.ShapeDtypeStruct((rows, width), BF16),
        scratch_shapes=[pltpu.VMEM((here, width), BF16), pltpu.SemaphoreType.DMA(())],
        input_output_aliases={len(inputs): 0} if before else {},
    )(*inputs, *before)


def on_device(
    edge_feats,
    cotangent,
    down_weight,
    up_weight,
    inner_weight,
    outer_weight,
    angular,
    reverse,
    sources,
    counts,
):
    lane_count = lax.axis_size("narrow")
    top_bit = lax.axis_size("cluster") // 2
    me = lax.axis_index("narrow")
    local_blocks, slots = sources.shape
    local_edges = edge_feats.shape[0]
    block = local_edges // local_blocks
    groups = local_blocks // 2
    packed_rows = local_edges // 2
    down_trans = down_weight.T

    live = lax.broadcasted_iota(jnp.int32, sources.shape, 1) < counts[:, None]
    local = sources % (local_blocks * lane_count)
    spot = (local // local_blocks ^ me) * local_blocks + local % local_blocks
    odd = lax.broadcasted_iota(jnp.int32, sources.shape, 0) % 2
    turned = jnp.where(spot % 2 == odd, 0, lane_count * groups)
    index = jnp.where(live, turned + spot // 2, 2 * lane_count * groups).reshape(-1)

    slot = reverse % local_edges
    place = (slot // block % 2) * packed_rows + slot // (2 * block) * block + slot % block
    place_row = place.reshape(1, local_edges)
    place = place.reshape(groups, 2 * block)

    cuts = [0, groups * 8 // 16, groups * 13 // 16, groups]
    parts = [end - start for start, end in zip(cuts, cuts[1:])]
    sizes = [parts[0], groups - parts[0]]

    pre_down, *trip = down(edge_feats, down_trans, block, [groups])
    angle_in, angle_out, spot, token = ahead(angular, place_row, [trip[0], index, place], block)
    pieces = {0: trip}
    bits = [1 << i for i in range(lane_count.bit_length() - 1)]
    for bit in reversed(bits):
        if bit > 1:
            pieces.update({d ^ bit: [swapped(half, "narrow", bit) for half in piece] for d, piece in pieces.items()})
    more = {d ^ 1: [swapped(half, "narrow", 1) for half in piece] for d, piece in pieces.items() if d + 2 < lane_count}
    here, gone = pieces[lane_count - 2], []
    for i in range(len(here)):
        here[i], token, *gone = lax.optimization_barrier((here[i], token, *gone))
        gone.append(swapped(here[i], "narrow", 1))
    pieces.update(more)
    pieces[lane_count - 1] = gone
    pieces = [pieces[d] for d in range(lane_count)]
    trip_own, early, late = triplet(index, spot, place, angle_in, pieces, token, block, slots, sizes)
    early = swapped(early, "cluster", top_bit)
    base, slope, wi, wo = gate(edge_feats, trip_own, up_weight, inner_weight[0], outer_weight[0], block)
    early, late, base, slope = lax.optimization_barrier((early, late, base, slope))
    late = swapped(late, "cluster", top_bit)
    done, grads, far = [], [], []
    for first, part in zip(cuts, parts):
        output, grad, sent = layer(
            base,
            cotangent,
            late if first else early,
            up_weight,
            wi,
            wo,
            done,
            block,
            first,
            part,
            first - parts[0] if first else 0,
        )
        done = [output]
        grads.append(grad)
        far.append(swapped(sent, "cluster", top_bit))
    near, spot = near_part(slope, up_weight, place, grads, block)
    types = [BF16 if d % 2 else F32 for d in range(lane_count)]
    sums = scatter(index, place, spot, angle_out, near, far, types, sizes, block, slots)
    sums = {d: sums[len(sizes) * d : len(sizes) * (d + 1)] for d in range(lane_count)}
    terms = [[half] for half in sums[0]]
    for bit in bits:
        for d in range(lane_count - bit, -1, -2 * bit):
            got = [swapped(half.astype(BF16), "narrow", bit) for half in sums[d]]
            if d == bit:
                terms = [term + [half] for term, half in zip(terms, got)]
            else:
                sums[d ^ bit] = [held + half.astype(F32) for held, half in zip(sums[d ^ bit], got)]
    grad_x = last(pre_down, grads[:1], down_trans, terms[0], [], block, 0)
    grad_x = last(pre_down, grads[1:], down_trans, terms[1], [grad_x], block, 2 * sizes[0] * block)
    return (output, grad_x)


def solution(mesh):
    in_specs = (
        P(("cluster", "narrow"), None),
        P(("cluster", "narrow"), None),
        P(),
        P(),
        P(),
        P(),
        P(("cluster", "narrow"), None, None),
        P(("cluster", "narrow")),
        P(("cluster", "narrow"), None),
        P(("cluster", "narrow")),
    )
    out_specs = (P(("cluster", "narrow"), None), P(("cluster", "narrow"), None))
    return jax.shard_map(
        on_device, mesh=mesh, in_specs=in_specs, out_specs=out_specs, check_vma=False
    )
```

```python
import functools

import jax
import jax.numpy as jnp
from jax import lax
from jax.experimental import pallas as pl
from jax.experimental.pallas import tpu as pltpu
from jax.sharding import PartitionSpec as P

ROOT_HALF = 0.7071067811865476
MIB = 1 << 20
F32 = jnp.float32
BF16 = jnp.bfloat16
VMEM = pl.BlockSpec(memory_space=pltpu.VMEM)
SMEM = pl.BlockSpec(memory_space=pltpu.SMEM)
ANY = pl.BlockSpec(memory_space=pl.ANY)
HBM = pl.BlockSpec(memory_space=pltpu.HBM)


def dot(left, right):
    return jnp.dot(left, right, preferred_element_type=F32)


def dot_trans(left, right):
    return lax.dot_general(left, right, (((1,), (1,)), ((), ())), preferred_element_type=F32)


def swapped(array, axis, bit):
    return lax.ppermute(array, axis, [(i, i ^ bit) for i in range(lax.axis_size(axis))])


def left_lanes(shape):
    return lax.broadcasted_iota(jnp.int32, shape, 1) < shape[1] // 2


def turn(values):
    return pltpu.roll(values, values.shape[1] // 2, 1)


def split_pairs(rows, block):
    parts = rows.reshape(-1, 2, block, rows.shape[-1])
    return parts[:, 0].reshape(-1, rows.shape[-1]), parts[:, 1].reshape(-1, rows.shape[-1])


def join_pairs(even, odd, block):
    width = even.shape[-1]
    both = jnp.concatenate([even.reshape(-1, 1, block, width), odd.reshape(-1, 1, block, width)], axis=1)
    return both.reshape(-1, width)


def padded(weight):
    none = jnp.zeros_like(weight)
    return jnp.concatenate([weight, none], axis=0), jnp.concatenate([none, weight], axis=0)


def call(kernel, name, limit, flops, moved, **more):
    return pl.pallas_call(
        kernel,
        compiler_params=pltpu.CompilerParams(vmem_limit_bytes=limit),
        cost_estimate=pl.CostEstimate(flops=flops, bytes_accessed=moved, transcendentals=0),
        name=name,
        **more,
    )


def down_kernel(block, x_ref, wt_ref, pre_ref, *refs):
    trip_refs, (x_held, wt_held, sems) = refs[:-3], refs[-3:]
    copies = [
        pltpu.make_async_copy(x_ref, x_held, sems.at[0]),
        pltpu.make_async_copy(wt_ref, wt_held, sems.at[1]),
    ]
    for copy in copies:
        copy.start()
    for copy in copies:
        copy.wait()
    pre = project(x_held[...], wt_held[...], block)
    pre_ref[...] = pre
    trip = (pre * (0.5 * jnp.tanh(0.5 * pre) + 0.5)).astype(BF16)
    first = 0
    for trip_ref in trip_refs:
        trip_ref[...] = trip[first : first + trip_ref.shape[0]]
        first += trip_ref.shape[0]


def down(x, wt, block, halves):
    rows, width = x.shape
    lanes = 2 * wt.shape[0]
    return call(
        functools.partial(down_kernel, block),
        "down",
        12 * MIB,
        2 * rows * width * lanes,
        2 * rows * width,
        in_specs=[HBM] * 2,
        out_specs=[VMEM] * (1 + len(halves)),
        out_shape=[jax.ShapeDtypeStruct((rows // 2, lanes), F32)]
        + [jax.ShapeDtypeStruct((half * block, lanes), BF16) for half in halves],
        scratch_shapes=[
            pltpu.VMEM(x.shape, BF16),
            pltpu.VMEM(wt.shape, BF16),
            pltpu.SemaphoreType.DMA((2,)),
        ],
    )(*[pltpu.with_memory_space_constraint(array, pltpu.HBM) for array in (x, wt)])


def ahead_kernel(block, slots, angle_ref, row_ref, *refs):
    in_ref, spot_ref, token_ref, rows_ref, pair_ref = refs[-5:]
    lanes = 2 * block
    half = block // 2
    mask = left_lanes((half, lanes))
    token_ref[...] = jnp.zeros(token_ref.shape, BF16)

    def pair(m, carry):
        for k in range(2):
            wide = angle_ref[2 * m + k].astype(F32)
            for t in range(half):
                rows_ref[k, t * slots : (t + 1) * slots, :] = wide[:, t * lanes : (t + 1) * lanes]
            for s in range(0, slots, 2):
                first = rows_ref[k, pl.ds(s, half, stride=slots), :]
                second = rows_ref[k, pl.ds(s + 1, half, stride=slots), :]
                pair_ref[k, s // 2, pl.ds(0, half, stride=2), :] = jnp.where(mask, first, turn(second))
                pair_ref[k, s // 2, pl.ds(1, half, stride=2), :] = jnp.where(mask, turn(first), second)
        for p in range(slots // 2):
            first, second = pair_ref[0, p], pair_ref[1, p]
            in_ref[2 * m, :, p * lanes : (p + 1) * lanes] = first.astype(BF16)
            in_ref[2 * m + 1, :, p * lanes : (p + 1) * lanes] = second.astype(BF16)
        return carry

    lax.fori_loop(0, angle_ref.shape[0] // 2, pair, 0, unroll=2)
    folded = spot_ref.shape[0]
    row = lax.rem(row_ref[...], folded)
    tile = folded // 4
    for start in range(0, folded, tile):
        spot = lax.broadcasted_iota(jnp.int32, (tile, row.shape[1]), 0) + start
        spot_ref[start : start + tile, :] = (spot == row).astype(F32).astype(BF16)


def ahead(angular, row, after, block):
    blocks, slots, _ = angular.shape
    edges = row.shape[1]
    lanes = 2 * block
    return call(
        functools.partial(ahead_kernel, block, slots),
        "ahead",
        20 * MIB,
        0,
        8 * angular.size * 2,
        in_specs=[VMEM, VMEM] + [ANY] * len(after),
        out_specs=[VMEM] * 3,
        out_shape=[
            jax.ShapeDtypeStruct((blocks, block, slots * block), BF16),
            jax.ShapeDtypeStruct((edges // 4, edges), BF16),
            jax.ShapeDtypeStruct((16, lanes), BF16),
        ],
        scratch_shapes=[
            pltpu.VMEM((2, slots * block // 2, lanes), F32),
            pltpu.VMEM((2, slots // 2, block, lanes), F32),
        ],
    )(angular, row, *after)


def beside_kernel(block, angle_ref, place_ref, *refs):
    out_ref, spot_ref, token_ref = refs[-3:]
    token_ref[...] = jnp.zeros(token_ref.shape, BF16)
    lanes = 2 * block

    def pair(m, carry):
        both = jnp.concatenate([angle_ref[2 * m], angle_ref[2 * m + 1]], axis=0)
        for p in range(both.shape[1] // lanes):
            out_ref[m, p * lanes : (p + 1) * lanes, :] = both[:, p * lanes : (p + 1) * lanes].T
        return carry

    lax.fori_loop(0, out_ref.shape[0], pair, 0, unroll=2)
    place = place_ref[...].T
    folded = spot_ref.shape[1]
    tile = 2 * block
    for m in range(out_ref.shape[0]):
        spot = lax.broadcasted_iota(jnp.int32, (tile, folded), 1)
        column = lax.rem(place[:, m : m + 1], folded)
        spot_ref[m * tile : (m + 1) * tile, :] = (spot == column).astype(F32).astype(BF16)


def beside(angles, place, after, block):
    blocks, _, width = angles.shape
    lanes = 2 * block
    edges = place.size
    return call(
        functools.partial(beside_kernel, block),
        "beside",
        16 * MIB,
        0,
        0,
        in_specs=[VMEM] * 2 + [ANY],
        out_specs=[VMEM] * 3,
        out_shape=[
            jax.ShapeDtypeStruct((blocks // 2, width, lanes), BF16),
            jax.ShapeDtypeStruct((edges, edges // 4), BF16),
            jax.ShapeDtypeStruct((16, lanes), BF16),
        ],
    )(angles, place, after)


def triplet_kernel(block, slots, pieces, halves, parts, *refs):
    index_ref, spot_ref, place_ref, angle_ref = refs[:4]
    piece_refs = refs[4 : 4 + halves * pieces]
    trip_ref = refs[5 + halves * pieces]
    sent_refs = refs[-1 - len(parts) : -1]
    held_ref = refs[-1]
    packed_rows, lanes = trip_ref.shape
    groups = packed_rows // block
    mask = left_lanes((block, lanes))

    at = 0
    for piece_ref in piece_refs:
        rows = piece_ref[...]
        here = rows.shape[0] // block
        held_ref[at : at + here] = rows.reshape(here, block, lanes)
        rows = turn(rows.astype(F32)).astype(BF16)
        held_ref[pieces * groups + at : pieces * groups + at + here] = rows.reshape(here, block, lanes)
        at += here
    held_ref[2 * pieces * groups] = jnp.zeros((block, lanes), BF16)

    def target(q, carry):
        sides = []
        for pair in range(2):
            base = (4 * q + 2 * pair) * slots
            picked = [
                jnp.where(mask, held_ref[index_ref[base + s]], held_ref[index_ref[base + slots + s]])
                for s in range(slots)
            ]
            sides.append(jnp.concatenate(picked, axis=0))
        matrix = angle_ref[pl.ds(4 * q, 4)].reshape(4 * block, slots * block)
        every = dot(matrix, jnp.concatenate(sides, axis=1))
        for pair in range(2):
            part = every[pair * 2 * block : (pair + 1) * 2 * block, pair * lanes : (pair + 1) * lanes]
            total = jnp.where(mask, part[:block], part[block:]).astype(BF16)
            trip_ref[pl.ds(pl.multiple_of((2 * q + pair) * block, block), block), :] = total
        return carry

    lax.fori_loop(0, groups // 2, target, 0, unroll=True)

    place = place_ref[...].T
    folded = packed_rows // 2
    spread = []
    wide_mask = left_lanes((2 * block, lanes))
    lane_side = jnp.where(wide_mask, 1.0, 0.0)
    for m in range(groups):
        rows = trip_ref[m * block : (m + 1) * block, :].astype(F32)
        other = turn(rows)
        both = jnp.concatenate([jnp.where(mask, rows, other), jnp.where(mask, other, rows)], axis=0)
        column = place[:, m : m + 1]
        side = jnp.where(column < packed_rows, 1.0, 0.0)
        column = jnp.where(column < packed_rows, column, column - packed_rows)
        both = jnp.where(side == lane_side, both, 0.0)
        sides = [jnp.where(column < folded, both, 0.0), jnp.where(column < folded, 0.0, both)]
        spread.append(jnp.concatenate(sides, axis=1).astype(BF16))
    sent = dot(spot_ref[...], jnp.concatenate(spread, axis=0)).astype(BF16)
    sent = jnp.concatenate([sent[:, :lanes], sent[:, lanes:]], axis=0)
    first = 0
    for sent_ref in sent_refs:
        sent_ref[...] = sent[first : first + sent_ref.shape[0]]
        first += sent_ref.shape[0]


def triplet(index, spot, place, angles, pieces, after, block, slots, parts):
    count, halves = len(pieces), len(pieces[0])
    pieces = [half for piece in pieces for half in piece]
    lanes = pieces[0].shape[1]
    packed_rows = sum(half.shape[0] for half in pieces) // count
    held = packed_rows // block * 2 * count + 1
    return call(
        functools.partial(triplet_kernel, block, slots, count, halves, parts),
        "triplet",
        6 * MIB + 2 * held * block * lanes,
        2 * packed_rows * slots * block * lanes,
        8 * MIB,
        in_specs=[SMEM] + [VMEM] * (3 + len(pieces)) + [ANY],
        out_specs=[VMEM] * (1 + len(parts)),
        out_shape=[jax.ShapeDtypeStruct((packed_rows, lanes), BF16)]
        + [jax.ShapeDtypeStruct((part * block, lanes), BF16) for part in parts],
        scratch_shapes=[pltpu.VMEM((held, block, lanes), BF16)],
    )(index, spot, place, angles, *pieces, after)


def gated(half_pre):
    lifted = 1.0 + jnp.tanh(half_pre)
    value = half_pre * lifted
    return value, lifted + value * (2.0 - lifted)


def pre_up(rows, up, block):
    up2 = jnp.concatenate([up, up], axis=0)
    mask = left_lanes(rows.shape)
    none = jnp.zeros(rows.shape, BF16)
    return dot(join_pairs(jnp.where(mask, rows, none), jnp.where(mask, none, rows), block), up2)


def project(rows, up, block):
    both = dot_trans(rows.astype(BF16), jnp.concatenate([up, up], axis=0))
    even, odd = split_pairs(both, block)
    return jnp.where(left_lanes(even.shape), even, odd)


def gate_kernel(block, tile, x_ref, ct_ref, own_ref, up_ref, wi_ref, wo_ref, base_ref, slope_ref, *refs):
    scaled_ref, wi_half_ref, wo_half_ref = refs
    up = up_ref[...] * 0.5
    wi_half_ref[...] = wi_ref[...] * 0.5
    wo_half_ref[...] = wo_ref[...] * 0.5
    for start in range(0, x_ref.shape[0], tile):
        rows = own_ref[start // 2 : (start + tile) // 2, :]
        value, slope = gated(pre_up(rows, up, block))
        wide = slice(start, start + tile)
        base_ref[wide, :] = x_ref[wide, :].astype(F32) * ROOT_HALF + value * 0.5
        slope_ref[wide, :] = slope.astype(BF16)
        scaled_ref[wide, :] = ct_ref[wide, :].astype(F32) * (0.5 * ROOT_HALF)


def gate(x, ct, own, up, wi, wo, block):
    rows, width = x.shape
    return call(
        functools.partial(gate_kernel, block, 8 * block),
        "gate",
        8 * MIB,
        2 * rows * width * own.shape[1],
        8 * rows * width,
        in_specs=[VMEM] * 6,
        out_specs=[VMEM] * 5,
        out_shape=[
            jax.ShapeDtypeStruct((rows, width), F32),
            jax.ShapeDtypeStruct((rows, width), BF16),
            jax.ShapeDtypeStruct((rows, width), F32),
            jax.ShapeDtypeStruct(wi.shape, BF16),
            jax.ShapeDtypeStruct(wo.shape, BF16),
        ],
    )(x, ct, own, up, wi, wo)


def layer_kernel(block, first, far_first, base_ref, scaled_ref, far_ref, up_ref, wi_ref, wo_ref, *refs):
    out_ref, grad_ref, send_ref, held_ref, sem = refs[-5:]
    rows = grad_ref.shape[0]
    wide = slice(first * 2 * block, first * 2 * block + rows)
    up = up_ref[...] * 0.5
    far = far_ref[far_first * block : far_first * block + rows // 2, :]
    far_value, far_slope = gated(pre_up(far, up, block))
    hidden = base_ref[wide, :] + far_value * 0.5
    wi, wo = wi_ref[...], wo_ref[...]
    in_value, in_slope = gated(dot(hidden.astype(BF16), wi))
    out_value, out_slope = gated(dot(in_value.astype(BF16), wo))
    held_ref[...] = ((hidden + out_value) * ROOT_HALF).astype(BF16)
    copy = pltpu.make_async_copy(held_ref, out_ref.at[wide, :], sem)
    copy.start()
    scaled = scaled_ref[wide, :]
    grad_out = (scaled * out_slope).astype(BF16)
    grad_in = (dot_trans(grad_out, wo) * in_slope).astype(BF16)
    half_grad = scaled + dot_trans(grad_in, wi)
    grad_ref[...] = (half_grad * (2.0 * ROOT_HALF)).astype(BF16)
    send_ref[...] = project(half_grad * far_slope, up, block).astype(BF16)
    copy.wait()


def layer(base, ct, far, up, wi, wo, before, block, first, part, far_first):
    rows, width = base.shape
    lanes = far.shape[1]
    return call(
        functools.partial(layer_kernel, block, first, far_first),
        "layer",
        32 * MIB,
        0,
        0,
        in_specs=[VMEM] * 6 + [HBM] * len(before),
        out_specs=[HBM, VMEM, VMEM],
        out_shape=[
            jax.ShapeDtypeStruct((rows, width), BF16),
            jax.ShapeDtypeStruct((part * 2 * block, width), BF16),
            jax.ShapeDtypeStruct((part * block, lanes), BF16),
        ],
        scratch_shapes=[pltpu.VMEM((part * 2 * block, width), BF16), pltpu.SemaphoreType.DMA(())],
        input_output_aliases={6 + i: i for i in range(len(before))},
    )(base, ct, far, up, wi, wo, *before)


def near_kernel(block, slope_ref, up_ref, *refs):
    near_ref = refs[-1]
    up = up_ref[...] * 0.5
    first = 0
    for grad_ref in refs[:-2]:
        rows = grad_ref.shape[0]
        both = grad_ref[...].astype(F32) * slope_ref[first : first + rows, :].astype(F32)
        near_ref[first // 2 : (first + rows) // 2, :] = project(both, up, block) * ROOT_HALF
        first += rows


def near_part(slope, up, grads, after, block):
    rows, width = slope.shape
    lanes = 2 * up.shape[0]
    return call(
        functools.partial(near_kernel, block),
        "near",
        8 * MIB,
        2 * rows * width * lanes,
        4 * rows * width,
        in_specs=[VMEM] * (2 + len(grads)) + [ANY],
        out_specs=VMEM,
        out_shape=jax.ShapeDtypeStruct((rows // 2, lanes), F32),
    )(slope, up, *grads, after)


def scatter_kernel(block, slots, pieces, chunks, index_ref, place_ref, spot_ref, angle_ref, near_ref, *refs):
    far_refs, out_refs = refs[:chunks], refs[chunks:-2]
    total_ref, grad_ref = refs[-2:]
    packed_rows, lanes = grad_ref.shape
    groups = packed_rows // block
    mask = left_lanes((block, lanes))
    total_ref[...] = jnp.zeros(total_ref.shape, F32)
    place = place_ref[...].T
    tile = 2 * block
    wide_mask = left_lanes((tile, lanes))
    lane_side = jnp.where(wide_mask, 1.0, 0.0)
    far = jnp.concatenate([far_ref[...] for far_ref in far_refs], axis=0)
    folded = packed_rows // 2
    far = jnp.concatenate([far[:folded], far[folded:]], axis=1)
    several = 4
    for start in range(0, groups, several):
        got = dot(spot_ref[start * tile : (start + several) * tile, :], far)
        for i, m in enumerate(range(start, start + several)):
            column = place[:, m : m + 1]
            side = jnp.where(column < packed_rows, 1.0, 0.0)
            column = jnp.where(column < packed_rows, column, column - packed_rows)
            mine = got[i * tile : (i + 1) * tile]
            mine = jnp.where(column < folded, mine[:, :lanes], mine[:, lanes:])
            mine = jnp.where(side == lane_side, mine, 0.0)
            mine = mine + turn(mine)
            at = m * block
            both = near_ref[at : at + block, :] + jnp.where(mask, mine[:block], mine[block:])
            grad_ref[at : at + block, :] = both.astype(BF16)
    none = jnp.zeros((block, lanes), BF16)

    def target(q, carry):
        sides = []
        for m in range(2):
            rows = grad_ref[pl.ds(pl.multiple_of((2 * q + m) * block, block), block), :]
            pair = jnp.concatenate([jnp.where(mask, rows, none), jnp.where(mask, none, rows)], axis=0)
            sides.append(jnp.concatenate([jnp.zeros_like(pair)] * m + [pair] + [jnp.zeros_like(pair)] * (1 - m), axis=1))
        matrix = jnp.concatenate([angle_ref[2 * q], angle_ref[2 * q + 1]], axis=1)
        every = dot(matrix, jnp.concatenate(sides, axis=0))
        for m in range(2):
            base = (2 * q + m) * (2 * slots)
            for s in range(slots):
                term = every[s * block : (s + 1) * block, m * lanes : (m + 1) * lanes]
                total_ref[index_ref[base + s]] += jnp.where(mask, term, 0.0)
                total_ref[index_ref[base + slots + s]] += jnp.where(mask, 0.0, term)
        return carry

    lax.fori_loop(0, groups // 2, target, 0, unroll=True)

    for piece in range(pieces):
        at = piece * groups
        for half in range(len(out_refs) // pieces):
            out_ref = out_refs[piece * (len(out_refs) // pieces) + half]
            rows = out_ref.shape[0]
            straight = total_ref[at : at + rows // block].reshape(rows, lanes)
            crossed = total_ref[pieces * groups + at : pieces * groups + at + rows // block].reshape(rows, lanes)
            out_ref[...] = (straight + turn(crossed)).astype(out_ref.dtype)
            at += rows // block


def scatter(index, place, spot, angles, near, far, types, halves, block, slots):
    chunks = len(far)
    packed_rows, lanes = near.shape
    pieces = len(types)
    held = 2 * pieces * (packed_rows // block) + 1
    outs = [jax.ShapeDtypeStruct((half * block, lanes), kind) for kind in types for half in halves]
    return call(
        functools.partial(scatter_kernel, block, slots, pieces, chunks),
        "scatter",
        16 * MIB + 4 * held * block * lanes,
        2 * packed_rows * slots * block * lanes,
        8 * MIB,
        in_specs=[SMEM] + [VMEM] * (4 + chunks),
        out_specs=[VMEM] * len(outs),
        out_shape=outs,
        scratch_shapes=[
            pltpu.VMEM((held, block, lanes), F32),
            pltpu.VMEM((packed_rows, lanes), BF16),
        ],
    )(index, place, spot, angles, near, *far)


def last_kernel(block, grads, terms, start, pre_ref, wt_ref, *refs):
    grad_refs, term_refs = refs[:grads], refs[grads : grads + terms]
    out_ref, held_ref, sem = refs[-3:]
    rows = held_ref.shape[0]
    thin = slice(start // 2, (start + rows) // 2)
    left, right = padded(wt_ref[...])
    total = term_refs[0][...].astype(F32)
    for ref in term_refs[1:]:
        total = total + ref[...].astype(F32)
    _, slope = gated(pre_ref[thin, :] * 0.5)
    grad = (total * (0.5 * slope)).astype(BF16)
    both = join_pairs(dot(grad, left), dot(grad, right), block)
    first = 0
    for grad_ref in grad_refs:
        here = slice(first, first + grad_ref.shape[0])
        held_ref[here, :] = (grad_ref[...].astype(F32) + both[here]).astype(BF16)
        first += grad_ref.shape[0]
    copy = pltpu.make_async_copy(held_ref, out_ref.at[start : start + rows, :], sem)
    copy.start()
    copy.wait()


def last(pre, grads, wt, terms, before, block, start):
    rows, width = 2 * pre.shape[0], wt.shape[1]
    here = 2 * terms[0].shape[0]
    inputs = [pre, wt, *grads, *terms]
    return call(
        functools.partial(last_kernel, block, len(grads), len(terms), start),
        "last",
        12 * MIB,
        0,
        0,
        in_specs=[VMEM] * len(inputs) + [HBM] * len(before),
        out_specs=HBM,
        out_shape=jax.ShapeDtypeStruct((rows, width), BF16),
        scratch_shapes=[pltpu.VMEM((here, width), BF16), pltpu.SemaphoreType.DMA(())],
        input_output_aliases={len(inputs): 0} if before else {},
    )(*inputs, *before)


def on_device(
    edge_feats,
    cotangent,
    down_weight,
    up_weight,
    inner_weight,
    outer_weight,
    angular,
    reverse,
    sources,
    counts,
):
    lane_count = lax.axis_size("narrow")
    top_bit = lax.axis_size("cluster") // 2
    me = lax.axis_index("narrow")
    local_blocks, slots = sources.shape
    local_edges = edge_feats.shape[0]
    block = local_edges // local_blocks
    groups = local_blocks // 2
    packed_rows = local_edges // 2
    down_trans = down_weight.T

    live = lax.broadcasted_iota(jnp.int32, sources.shape, 1) < counts[:, None]
    local = sources % (local_blocks * lane_count)
    spot = (local // local_blocks ^ me) * local_blocks + local % local_blocks
    odd = lax.broadcasted_iota(jnp.int32, sources.shape, 0) % 2
    turned = jnp.where(spot % 2 == odd, 0, lane_count * groups)
    index = jnp.where(live, turned + spot // 2, 2 * lane_count * groups).reshape(-1)

    slot = reverse % local_edges
    place = (slot // block % 2) * packed_rows + slot // (2 * block) * block + slot % block
    place_row = place.reshape(1, local_edges)
    place = place.reshape(groups, 2 * block)

    cuts = [0, groups * 9 // 16, groups * 13 // 16, groups]
    parts = [end - start for start, end in zip(cuts, cuts[1:])]
    sizes = [parts[0], groups - parts[0]]

    pre_down, *trip = down(edge_feats, down_trans, block, [groups])
    angle_in, spot, token = ahead(angular, place_row, [trip[0], index, place], block)
    pieces = {0: trip}
    bits = [1 << i for i in range(lane_count.bit_length() - 1)]
    for bit in reversed(bits):
        if bit > 1:
            pieces.update({d ^ bit: [swapped(half, "narrow", bit) for half in piece] for d, piece in pieces.items()})
    more = {d ^ 1: [swapped(half, "narrow", 1) for half in piece] for d, piece in pieces.items() if d + 2 < lane_count}
    here, gone = pieces[lane_count - 2], []
    for i in range(len(here)):
        here[i], token, *gone = lax.optimization_barrier((here[i], token, *gone))
        gone.append(swapped(here[i], "narrow", 1))
    pieces.update(more)
    pieces[lane_count - 1] = gone
    pieces = [pieces[d] for d in range(lane_count)]
    trip_own, early, late = triplet(index, spot, place, angle_in, pieces, token, block, slots, sizes)
    early = swapped(early, "cluster", top_bit)
    base, slope, scaled, wi, wo = gate(
        edge_feats, cotangent, trip_own, up_weight, inner_weight[0], outer_weight[0], block
    )
    angle_out, spot, token = beside(angle_in, place, trip_own, block)
    late, base, slope, token = lax.optimization_barrier((late, base, slope, token))
    late = swapped(late, "cluster", top_bit)
    done, grads, far = [], [], []
    for first, part in zip(cuts, parts):
        output, grad, sent = layer(
            base,
            scaled,
            late if first else early,
            up_weight,
            wi,
            wo,
            done,
            block,
            first,
            part,
            first - parts[0] if first else 0,
        )
        done = [output]
        grads.append(grad)
        far.append(swapped(sent, "cluster", top_bit))
    near = near_part(slope, up_weight, grads, token, block)
    types = [BF16 if d % 2 else F32 for d in range(lane_count)]
    sums = scatter(index, place, spot, angle_out, near, far, types, sizes, block, slots)
    sums = {d: sums[len(sizes) * d : len(sizes) * (d + 1)] for d in range(lane_count)}
    terms = [[half] for half in sums[0]]
    for bit in bits:
        for d in range(lane_count - bit, -1, -2 * bit):
            got = [swapped(half.astype(BF16), "narrow", bit) for half in sums[d]]
            if d == bit:
                terms = [term + [half] for term, half in zip(terms, got)]
            else:
                sums[d ^ bit] = [held + half.astype(F32) for held, half in zip(sums[d ^ bit], got)]
    grad_x = last(pre_down, grads[:1], down_trans, terms[0], [], block, 0)
    grad_x = last(pre_down, grads[1:], down_trans, terms[1], [grad_x], block, 2 * sizes[0] * block)
    return (output, grad_x)


def solution(mesh):
    in_specs = (
        P(("cluster", "narrow"), None),
        P(("cluster", "narrow"), None),
        P(),
        P(),
        P(),
        P(),
        P(("cluster", "narrow"), None, None),
        P(("cluster", "narrow")),
        P(("cluster", "narrow"), None),
        P(("cluster", "narrow")),
    )
    out_specs = (P(("cluster", "narrow"), None), P(("cluster", "narrow"), None))
    return jax.shard_map(
        on_device, mesh=mesh, in_specs=in_specs, out_specs=out_specs, check_vma=False
    )
```

```python
import functools

import jax
import jax.numpy as jnp
from jax import lax
from jax.experimental import pallas as pl
from jax.experimental.pallas import tpu as pltpu
from jax.sharding import PartitionSpec as P

ROOT_HALF = 0.7071067811865476
MIB = 1 << 20
F32 = jnp.float32
BF16 = jnp.bfloat16
VMEM = pl.BlockSpec(memory_space=pltpu.VMEM)
SMEM = pl.BlockSpec(memory_space=pltpu.SMEM)
ANY = pl.BlockSpec(memory_space=pl.ANY)
HBM = pl.BlockSpec(memory_space=pltpu.HBM)


def dot(left, right):
    return jnp.dot(left, right, preferred_element_type=F32)


def dot_trans(left, right):
    return lax.dot_general(left, right, (((1,), (1,)), ((), ())), preferred_element_type=F32)


def swapped(array, axis, bit):
    return lax.ppermute(array, axis, [(i, i ^ bit) for i in range(lax.axis_size(axis))])


def left_lanes(shape):
    return lax.broadcasted_iota(jnp.int32, shape, 1) < shape[1] // 2


def turn(values):
    return pltpu.roll(values, values.shape[1] // 2, 1)


def split_pairs(rows, block):
    parts = rows.reshape(-1, 2, block, rows.shape[-1])
    return parts[:, 0].reshape(-1, rows.shape[-1]), parts[:, 1].reshape(-1, rows.shape[-1])


def join_pairs(even, odd, block):
    width = even.shape[-1]
    both = jnp.concatenate([even.reshape(-1, 1, block, width), odd.reshape(-1, 1, block, width)], axis=1)
    return both.reshape(-1, width)


def padded(weight):
    none = jnp.zeros_like(weight)
    return jnp.concatenate([weight, none], axis=0), jnp.concatenate([none, weight], axis=0)


def call(kernel, name, limit, flops, moved, **more):
    return pl.pallas_call(
        kernel,
        compiler_params=pltpu.CompilerParams(vmem_limit_bytes=limit),
        cost_estimate=pl.CostEstimate(flops=flops, bytes_accessed=moved, transcendentals=0),
        name=name,
        **more,
    )


def down_kernel(block, x_ref, wt_ref, pre_ref, *refs):
    trip_refs, (x_held, wt_held, sems) = refs[:-3], refs[-3:]
    copies = [
        pltpu.make_async_copy(x_ref, x_held, sems.at[0]),
        pltpu.make_async_copy(wt_ref, wt_held, sems.at[1]),
    ]
    for copy in copies:
        copy.start()
    for copy in copies:
        copy.wait()
    pre = project(x_held[...], wt_held[...], block)
    pre_ref[...] = pre
    trip = (pre * (0.5 * jnp.tanh(0.5 * pre) + 0.5)).astype(BF16)
    first = 0
    for trip_ref in trip_refs:
        trip_ref[...] = trip[first : first + trip_ref.shape[0]]
        first += trip_ref.shape[0]


def down(x, wt, block, halves):
    rows, width = x.shape
    lanes = 2 * wt.shape[0]
    return call(
        functools.partial(down_kernel, block),
        "down",
        12 * MIB,
        2 * rows * width * lanes,
        2 * rows * width,
        in_specs=[HBM] * 2,
        out_specs=[VMEM] * (1 + len(halves)),
        out_shape=[jax.ShapeDtypeStruct((rows // 2, lanes), F32)]
        + [jax.ShapeDtypeStruct((half * block, lanes), BF16) for half in halves],
        scratch_shapes=[
            pltpu.VMEM(x.shape, BF16),
            pltpu.VMEM(wt.shape, BF16),
            pltpu.SemaphoreType.DMA((2,)),
        ],
    )(*[pltpu.with_memory_space_constraint(array, pltpu.HBM) for array in (x, wt)])


def ahead_kernel(block, slots, angle_ref, row_ref, *refs):
    in_ref, spot_ref, token_ref, rows_ref, pair_ref = refs[-5:]
    lanes = 2 * block
    half = block // 2
    mask = left_lanes((half, lanes))
    token_ref[...] = jnp.zeros(token_ref.shape, BF16)

    def pair(m, carry):
        for k in range(2):
            wide = angle_ref[2 * m + k].astype(F32)
            for t in range(half):
                rows_ref[k, t * slots : (t + 1) * slots, :] = wide[:, t * lanes : (t + 1) * lanes]
            for s in range(0, slots, 2):
                first = rows_ref[k, pl.ds(s, half, stride=slots), :]
                second = rows_ref[k, pl.ds(s + 1, half, stride=slots), :]
                pair_ref[k, s // 2, pl.ds(0, half, stride=2), :] = jnp.where(mask, first, turn(second))
                pair_ref[k, s // 2, pl.ds(1, half, stride=2), :] = jnp.where(mask, turn(first), second)
        for p in range(slots // 2):
            first, second = pair_ref[0, p], pair_ref[1, p]
            in_ref[2 * m, :, p * lanes : (p + 1) * lanes] = first.astype(BF16)
            in_ref[2 * m + 1, :, p * lanes : (p + 1) * lanes] = second.astype(BF16)
        return carry

    lax.fori_loop(0, angle_ref.shape[0] // 2, pair, 0, unroll=2)
    folded = spot_ref.shape[0]
    row = lax.rem(row_ref[...], folded)
    tile = folded // 4
    for start in range(0, folded, tile):
        spot = lax.broadcasted_iota(jnp.int32, (tile, row.shape[1]), 0) + start
        spot_ref[start : start + tile, :] = (spot == row).astype(F32).astype(BF16)


def ahead(angular, row, after, block):
    blocks, slots, _ = angular.shape
    edges = row.shape[1]
    lanes = 2 * block
    return call(
        functools.partial(ahead_kernel, block, slots),
        "ahead",
        20 * MIB,
        0,
        8 * angular.size * 2,
        in_specs=[VMEM, VMEM] + [ANY] * len(after),
        out_specs=[VMEM] * 3,
        out_shape=[
            jax.ShapeDtypeStruct((blocks, block, slots * block), BF16),
            jax.ShapeDtypeStruct((edges // 4, edges), BF16),
            jax.ShapeDtypeStruct((16, lanes), BF16),
        ],
        scratch_shapes=[
            pltpu.VMEM((2, slots * block // 2, lanes), F32),
            pltpu.VMEM((2, slots // 2, block, lanes), F32),
        ],
    )(angular, row, *after)


def beside_kernel(block, angle_ref, place_ref, *refs):
    out_ref, spot_ref, token_ref = refs[-3:]
    token_ref[...] = jnp.zeros(token_ref.shape, BF16)
    lanes = 2 * block

    def pair(m, carry):
        both = jnp.concatenate([angle_ref[2 * m], angle_ref[2 * m + 1]], axis=0)
        for p in range(both.shape[1] // lanes):
            out_ref[m, p * lanes : (p + 1) * lanes, :] = both[:, p * lanes : (p + 1) * lanes].T
        return carry

    lax.fori_loop(0, out_ref.shape[0], pair, 0, unroll=2)
    place = place_ref[...].T
    folded = spot_ref.shape[1]
    tile = 2 * block
    for m in range(out_ref.shape[0]):
        spot = lax.broadcasted_iota(jnp.int32, (tile, folded), 1)
        column = lax.rem(place[:, m : m + 1], folded)
        spot_ref[m * tile : (m + 1) * tile, :] = (spot == column).astype(F32).astype(BF16)


def beside(angles, place, after, block):
    blocks, _, width = angles.shape
    lanes = 2 * block
    edges = place.size
    return call(
        functools.partial(beside_kernel, block),
        "beside",
        16 * MIB,
        0,
        0,
        in_specs=[VMEM] * 2 + [ANY],
        out_specs=[VMEM] * 3,
        out_shape=[
            jax.ShapeDtypeStruct((blocks // 2, width, lanes), BF16),
            jax.ShapeDtypeStruct((edges, edges // 4), BF16),
            jax.ShapeDtypeStruct((16, lanes), BF16),
        ],
    )(angles, place, after)


def triplet_kernel(block, slots, pieces, halves, parts, *refs):
    index_ref, spot_ref, place_ref, angle_ref = refs[:4]
    piece_refs = refs[4 : 4 + halves * pieces]
    trip_ref = refs[5 + halves * pieces]
    sent_refs = refs[-1 - len(parts) : -1]
    held_ref = refs[-1]
    packed_rows, lanes = trip_ref.shape
    groups = packed_rows // block
    mask = left_lanes((block, lanes))

    at = 0
    for piece_ref in piece_refs:
        rows = piece_ref[...]
        here = rows.shape[0] // block
        held_ref[at : at + here] = rows.reshape(here, block, lanes)
        rows = turn(rows.astype(F32)).astype(BF16)
        held_ref[pieces * groups + at : pieces * groups + at + here] = rows.reshape(here, block, lanes)
        at += here
    held_ref[2 * pieces * groups] = jnp.zeros((block, lanes), BF16)

    def target(q, carry):
        sides = []
        for pair in range(2):
            base = (4 * q + 2 * pair) * slots
            picked = [
                jnp.where(mask, held_ref[index_ref[base + s]], held_ref[index_ref[base + slots + s]])
                for s in range(slots)
            ]
            sides.append(jnp.concatenate(picked, axis=0))
        matrix = angle_ref[pl.ds(4 * q, 4)].reshape(4 * block, slots * block)
        every = dot(matrix, jnp.concatenate(sides, axis=1))
        for pair in range(2):
            part = every[pair * 2 * block : (pair + 1) * 2 * block, pair * lanes : (pair + 1) * lanes]
            total = jnp.where(mask, part[:block], part[block:]).astype(BF16)
            trip_ref[pl.ds(pl.multiple_of((2 * q + pair) * block, block), block), :] = total
        return carry

    lax.fori_loop(0, groups // 2, target, 0, unroll=True)

    place = place_ref[...].T
    folded = packed_rows // 2
    spread = []
    wide_mask = left_lanes((2 * block, lanes))
    lane_side = jnp.where(wide_mask, 1.0, 0.0)
    for m in range(groups):
        rows = trip_ref[m * block : (m + 1) * block, :].astype(F32)
        other = turn(rows)
        both = jnp.concatenate([jnp.where(mask, rows, other), jnp.where(mask, other, rows)], axis=0)
        column = place[:, m : m + 1]
        side = jnp.where(column < packed_rows, 1.0, 0.0)
        column = jnp.where(column < packed_rows, column, column - packed_rows)
        both = jnp.where(side == lane_side, both, 0.0)
        sides = [jnp.where(column < folded, both, 0.0), jnp.where(column < folded, 0.0, both)]
        spread.append(jnp.concatenate(sides, axis=1).astype(BF16))
    sent = dot(spot_ref[...], jnp.concatenate(spread, axis=0)).astype(BF16)
    sent = jnp.concatenate([sent[:, :lanes], sent[:, lanes:]], axis=0)
    first = 0
    for sent_ref in sent_refs:
        sent_ref[...] = sent[first : first + sent_ref.shape[0]]
        first += sent_ref.shape[0]


def triplet(index, spot, place, angles, pieces, after, block, slots, parts):
    count, halves = len(pieces), len(pieces[0])
    pieces = [half for piece in pieces for half in piece]
    lanes = pieces[0].shape[1]
    packed_rows = sum(half.shape[0] for half in pieces) // count
    held = packed_rows // block * 2 * count + 1
    return call(
        functools.partial(triplet_kernel, block, slots, count, halves, parts),
        "triplet",
        6 * MIB + 2 * held * block * lanes,
        2 * packed_rows * slots * block * lanes,
        8 * MIB,
        in_specs=[SMEM] + [VMEM] * (3 + len(pieces)) + [ANY],
        out_specs=[VMEM] * (1 + len(parts)),
        out_shape=[jax.ShapeDtypeStruct((packed_rows, lanes), BF16)]
        + [jax.ShapeDtypeStruct((part * block, lanes), BF16) for part in parts],
        scratch_shapes=[pltpu.VMEM((held, block, lanes), BF16)],
    )(index, spot, place, angles, *pieces, after)


def gated(half_pre):
    lifted = 1.0 + jnp.tanh(half_pre)
    value = half_pre * lifted
    return value, lifted + value * (2.0 - lifted)


def pre_up(rows, up, block):
    up2 = jnp.concatenate([up, up], axis=0)
    mask = left_lanes(rows.shape)
    none = jnp.zeros(rows.shape, BF16)
    return dot(join_pairs(jnp.where(mask, rows, none), jnp.where(mask, none, rows), block), up2)


def project(rows, up, block):
    both = dot_trans(rows.astype(BF16), jnp.concatenate([up, up], axis=0))
    even, odd = split_pairs(both, block)
    return jnp.where(left_lanes(even.shape), even, odd)


def gate_kernel(block, tile, x_ref, ct_ref, own_ref, up_ref, wi_ref, wo_ref, base_ref, slope_ref, *refs):
    scaled_ref, wi_half_ref, wo_half_ref = refs
    up = up_ref[...] * 0.5
    wi_half_ref[...] = wi_ref[...] * 0.5
    wo_half_ref[...] = wo_ref[...] * 0.5
    for start in range(0, x_ref.shape[0], tile):
        rows = own_ref[start // 2 : (start + tile) // 2, :]
        value, slope = gated(pre_up(rows, up, block))
        wide = slice(start, start + tile)
        base_ref[wide, :] = x_ref[wide, :].astype(F32) * ROOT_HALF + value * 0.5
        slope_ref[wide, :] = slope.astype(BF16)
        scaled_ref[wide, :] = ct_ref[wide, :].astype(F32) * (0.5 * ROOT_HALF)


def gate(x, ct, own, up, wi, wo, block):
    rows, width = x.shape
    return call(
        functools.partial(gate_kernel, block, 8 * block),
        "gate",
        8 * MIB,
        2 * rows * width * own.shape[1],
        8 * rows * width,
        in_specs=[VMEM] * 6,
        out_specs=[VMEM] * 5,
        out_shape=[
            jax.ShapeDtypeStruct((rows, width), F32),
            jax.ShapeDtypeStruct((rows, width), BF16),
            jax.ShapeDtypeStruct((rows, width), F32),
            jax.ShapeDtypeStruct(wi.shape, BF16),
            jax.ShapeDtypeStruct(wo.shape, BF16),
        ],
    )(x, ct, own, up, wi, wo)


def layer_kernel(block, first, far_first, base_ref, scaled_ref, far_ref, up_ref, wi_ref, wo_ref, *refs):
    out_ref, grad_ref, send_ref, held_ref, sem = refs[-5:]
    rows = grad_ref.shape[0]
    wide = slice(first * 2 * block, first * 2 * block + rows)
    up = up_ref[...] * 0.5
    far = far_ref[far_first * block : far_first * block + rows // 2, :]
    far_value, far_slope = gated(pre_up(far, up, block))
    hidden = base_ref[wide, :] + far_value * 0.5
    wi, wo = wi_ref[...], wo_ref[...]
    in_value, in_slope = gated(dot(hidden.astype(BF16), wi))
    out_value, out_slope = gated(dot(in_value.astype(BF16), wo))
    held_ref[...] = ((hidden + out_value) * ROOT_HALF).astype(BF16)
    copy = pltpu.make_async_copy(held_ref, out_ref.at[wide, :], sem)
    copy.start()
    scaled = scaled_ref[wide, :]
    grad_out = (scaled * out_slope).astype(BF16)
    grad_in = (dot_trans(grad_out, wo) * in_slope).astype(BF16)
    half_grad = scaled + dot_trans(grad_in, wi)
    grad_ref[...] = (half_grad * (2.0 * ROOT_HALF)).astype(BF16)
    send_ref[...] = project(half_grad * far_slope, up, block).astype(BF16)
    copy.wait()


def layer(base, ct, far, up, wi, wo, before, block, first, part, far_first):
    rows, width = base.shape
    lanes = far.shape[1]
    return call(
        functools.partial(layer_kernel, block, first, far_first),
        "layer",
        32 * MIB,
        0,
        0,
        in_specs=[VMEM] * 6 + [HBM] * len(before),
        out_specs=[HBM, VMEM, VMEM],
        out_shape=[
            jax.ShapeDtypeStruct((rows, width), BF16),
            jax.ShapeDtypeStruct((part * 2 * block, width), BF16),
            jax.ShapeDtypeStruct((part * block, lanes), BF16),
        ],
        scratch_shapes=[pltpu.VMEM((part * 2 * block, width), BF16), pltpu.SemaphoreType.DMA(())],
        input_output_aliases={6 + i: i for i in range(len(before))},
    )(base, ct, far, up, wi, wo, *before)


def near_kernel(block, slope_ref, up_ref, *refs):
    near_ref = refs[-1]
    up = up_ref[...] * 0.5
    first = 0
    for grad_ref in refs[:-2]:
        rows = grad_ref.shape[0]
        both = grad_ref[...].astype(F32) * slope_ref[first : first + rows, :].astype(F32)
        near_ref[first // 2 : (first + rows) // 2, :] = project(both, up, block) * ROOT_HALF
        first += rows


def near_part(slope, up, grads, after, block):
    rows, width = slope.shape
    lanes = 2 * up.shape[0]
    return call(
        functools.partial(near_kernel, block),
        "near",
        8 * MIB,
        2 * rows * width * lanes,
        4 * rows * width,
        in_specs=[VMEM] * (2 + len(grads)) + [ANY],
        out_specs=VMEM,
        out_shape=jax.ShapeDtypeStruct((rows // 2, lanes), F32),
    )(slope, up, *grads, after)


def scatter_kernel(block, slots, pieces, chunks, index_ref, place_ref, spot_ref, angle_ref, near_ref, *refs):
    far_refs, out_refs = refs[:chunks], refs[chunks:-2]
    total_ref, grad_ref = refs[-2:]
    packed_rows, lanes = grad_ref.shape
    groups = packed_rows // block
    mask = left_lanes((block, lanes))
    total_ref[...] = jnp.zeros(total_ref.shape, F32)
    place = place_ref[...].T
    tile = 2 * block
    wide_mask = left_lanes((tile, lanes))
    lane_side = jnp.where(wide_mask, 1.0, 0.0)
    far = jnp.concatenate([far_ref[...] for far_ref in far_refs], axis=0)
    folded = packed_rows // 2
    far = jnp.concatenate([far[:folded], far[folded:]], axis=1)
    several = 4
    for start in range(0, groups, several):
        got = dot(spot_ref[start * tile : (start + several) * tile, :], far)
        for i, m in enumerate(range(start, start + several)):
            column = place[:, m : m + 1]
            side = jnp.where(column < packed_rows, 1.0, 0.0)
            column = jnp.where(column < packed_rows, column, column - packed_rows)
            mine = got[i * tile : (i + 1) * tile]
            mine = jnp.where(column < folded, mine[:, :lanes], mine[:, lanes:])
            mine = jnp.where(side == lane_side, mine, 0.0)
            mine = mine + turn(mine)
            at = m * block
            both = near_ref[at : at + block, :] + jnp.where(mask, mine[:block], mine[block:])
            grad_ref[at : at + block, :] = both.astype(BF16)
    none = jnp.zeros((block, lanes), BF16)

    def target(q, carry):
        sides = []
        for m in range(2):
            rows = grad_ref[pl.ds(pl.multiple_of((2 * q + m) * block, block), block), :]
            pair = jnp.concatenate([jnp.where(mask, rows, none), jnp.where(mask, none, rows)], axis=0)
            sides.append(jnp.concatenate([jnp.zeros_like(pair)] * m + [pair] + [jnp.zeros_like(pair)] * (1 - m), axis=1))
        matrix = jnp.concatenate([angle_ref[2 * q], angle_ref[2 * q + 1]], axis=1)
        every = dot(matrix, jnp.concatenate(sides, axis=0))
        for m in range(2):
            base = (2 * q + m) * (2 * slots)
            for s in range(slots):
                term = every[s * block : (s + 1) * block, m * lanes : (m + 1) * lanes]
                total_ref[index_ref[base + s]] += jnp.where(mask, term, 0.0)
                total_ref[index_ref[base + slots + s]] += jnp.where(mask, 0.0, term)
        return carry

    lax.fori_loop(0, groups // 2, target, 0, unroll=True)

    for piece in range(pieces):
        at = piece * groups
        for half in range(len(out_refs) // pieces):
            out_ref = out_refs[piece * (len(out_refs) // pieces) + half]
            rows = out_ref.shape[0]
            straight = total_ref[at : at + rows // block].reshape(rows, lanes)
            crossed = total_ref[pieces * groups + at : pieces * groups + at + rows // block].reshape(rows, lanes)
            out_ref[...] = (straight + turn(crossed)).astype(out_ref.dtype)
            at += rows // block


def scatter(index, place, spot, angles, near, far, types, halves, block, slots):
    chunks = len(far)
    packed_rows, lanes = near.shape
    pieces = len(types)
    held = 2 * pieces * (packed_rows // block) + 1
    outs = [jax.ShapeDtypeStruct((half * block, lanes), kind) for kind in types for half in halves]
    return call(
        functools.partial(scatter_kernel, block, slots, pieces, chunks),
        "scatter",
        16 * MIB + 4 * held * block * lanes,
        2 * packed_rows * slots * block * lanes,
        8 * MIB,
        in_specs=[SMEM] + [VMEM] * (4 + chunks),
        out_specs=[VMEM] * len(outs),
        out_shape=outs,
        scratch_shapes=[
            pltpu.VMEM((held, block, lanes), F32),
            pltpu.VMEM((packed_rows, lanes), BF16),
        ],
    )(index, place, spot, angles, near, *far)


def last_kernel(block, grads, terms, start, pre_ref, wt_ref, *refs):
    grad_refs, term_refs = refs[:grads], refs[grads : grads + terms]
    out_ref, held_ref, sems = refs[-3:]
    groups = held_ref.shape[0] // (2 * block)
    left, right = padded(wt_ref[...])
    grad_rows = jnp.concatenate([grad_ref[...] for grad_ref in grad_refs], axis=0)
    copies = []
    for i, (low, high) in enumerate([(0, (groups + 1) // 2), ((groups + 1) // 2, groups)]):
        thin = slice(low * block, high * block)
        wide = slice(2 * low * block, 2 * high * block)
        total = term_refs[0][thin, :].astype(F32)
        for ref in term_refs[1:]:
            total = total + ref[thin, :].astype(F32)
        _, slope = gated(pre_ref[start // 2 + low * block : start // 2 + high * block, :] * 0.5)
        grad = (total * (0.5 * slope)).astype(BF16)
        both = join_pairs(dot(grad, left), dot(grad, right), block)
        held_ref[wide, :] = (grad_rows[wide].astype(F32) + both).astype(BF16)
        there = out_ref.at[start + 2 * low * block : start + 2 * high * block, :]
        copies.append(pltpu.make_async_copy(held_ref.at[wide, :], there, sems.at[i]))
        copies[-1].start()
    for copy in copies:
        copy.wait()


def last(pre, grads, wt, terms, before, block, start):
    rows, width = 2 * pre.shape[0], wt.shape[1]
    here = 2 * terms[0].shape[0]
    inputs = [pre, wt, *grads, *terms]
    return call(
        functools.partial(last_kernel, block, len(grads), len(terms), start),
        "last",
        12 * MIB,
        0,
        0,
        in_specs=[VMEM] * len(inputs) + [HBM] * len(before),
        out_specs=HBM,
        out_shape=jax.ShapeDtypeStruct((rows, width), BF16),
        scratch_shapes=[pltpu.VMEM((here, width), BF16), pltpu.SemaphoreType.DMA((2,))],
        input_output_aliases={len(inputs): 0} if before else {},
    )(*inputs, *before)


def on_device(
    edge_feats,
    cotangent,
    down_weight,
    up_weight,
    inner_weight,
    outer_weight,
    angular,
    reverse,
    sources,
    counts,
):
    lane_count = lax.axis_size("narrow")
    top_bit = lax.axis_size("cluster") // 2
    me = lax.axis_index("narrow")
    local_blocks, slots = sources.shape
    local_edges = edge_feats.shape[0]
    block = local_edges // local_blocks
    groups = local_blocks // 2
    packed_rows = local_edges // 2
    down_trans = down_weight.T

    live = lax.broadcasted_iota(jnp.int32, sources.shape, 1) < counts[:, None]
    local = sources % (local_blocks * lane_count)
    spot = (local // local_blocks ^ me) * local_blocks + local % local_blocks
    odd = lax.broadcasted_iota(jnp.int32, sources.shape, 0) % 2
    turned = jnp.where(spot % 2 == odd, 0, lane_count * groups)
    index = jnp.where(live, turned + spot // 2, 2 * lane_count * groups).reshape(-1)

    slot = reverse % local_edges
    place = (slot // block % 2) * packed_rows + slot // (2 * block) * block + slot % block
    place_row = place.reshape(1, local_edges)
    place = place.reshape(groups, 2 * block)

    cuts = [0, groups * 9 // 16, groups * 13 // 16, groups]
    parts = [end - start for start, end in zip(cuts, cuts[1:])]
    sizes = [parts[0], groups - parts[0]]

    pre_down, *trip = down(edge_feats, down_trans, block, [groups])
    angle_in, spot, token = ahead(angular, place_row, [trip[0], index, place], block)
    pieces = {0: trip}
    bits = [1 << i for i in range(lane_count.bit_length() - 1)]
    for bit in reversed(bits):
        if bit > 1:
            pieces.update({d ^ bit: [swapped(half, "narrow", bit) for half in piece] for d, piece in pieces.items()})
    more = {d ^ 1: [swapped(half, "narrow", 1) for half in piece] for d, piece in pieces.items() if d + 2 < lane_count}
    here, gone = pieces[lane_count - 2], []
    for i in range(len(here)):
        here[i], token, *gone = lax.optimization_barrier((here[i], token, *gone))
        gone.append(swapped(here[i], "narrow", 1))
    pieces.update(more)
    pieces[lane_count - 1] = gone
    pieces = [pieces[d] for d in range(lane_count)]
    trip_own, early, late = triplet(index, spot, place, angle_in, pieces, token, block, slots, sizes)
    early = swapped(early, "cluster", top_bit)
    base, slope, scaled, wi, wo = gate(
        edge_feats, cotangent, trip_own, up_weight, inner_weight[0], outer_weight[0], block
    )
    angle_out, spot, token = beside(angle_in, place, trip_own, block)
    late, base, slope, token = lax.optimization_barrier((late, base, slope, token))
    late = swapped(late, "cluster", top_bit)
    done, grads, far = [], [], []
    for first, part in zip(cuts, parts):
        output, grad, sent = layer(
            base,
            scaled,
            late if first else early,
            up_weight,
            wi,
            wo,
            done,
            block,
            first,
            part,
            first - parts[0] if first else 0,
        )
        done = [output]
        grads.append(grad)
        far.append(swapped(sent, "cluster", top_bit))
    near = near_part(slope, up_weight, grads, token, block)
    types = [BF16 if d % 2 else F32 for d in range(lane_count)]
    sums = scatter(index, place, spot, angle_out, near, far, types, sizes, block, slots)
    sums = {d: sums[len(sizes) * d : len(sizes) * (d + 1)] for d in range(lane_count)}
    terms = [[half] for half in sums[0]]
    for bit in bits:
        for d in range(lane_count - bit, -1, -2 * bit):
            got = [swapped(half.astype(BF16), "narrow", bit) for half in sums[d]]
            if d == bit:
                terms = [term + [half] for term, half in zip(terms, got)]
            else:
                sums[d ^ bit] = [held + half.astype(F32) for held, half in zip(sums[d ^ bit], got)]
    grad_x = last(pre_down, grads[:1], down_trans, terms[0], [], block, 0)
    grad_x = last(pre_down, grads[1:], down_trans, terms[1], [grad_x], block, 2 * sizes[0] * block)
    return (output, grad_x)


def solution(mesh):
    in_specs = (
        P(("cluster", "narrow"), None),
        P(("cluster", "narrow"), None),
        P(),
        P(),
        P(),
        P(),
        P(("cluster", "narrow"), None, None),
        P(("cluster", "narrow")),
        P(("cluster", "narrow"), None),
        P(("cluster", "narrow")),
    )
    out_specs = (P(("cluster", "narrow"), None), P(("cluster", "narrow"), None))
    return jax.shard_map(
        on_device, mesh=mesh, in_specs=in_specs, out_specs=out_specs, check_vma=False
    )
```
